128 devices in a mesh: sector: 16 (over y_hi, x, core), axial: 8 (over z, y_lo).
Axes of the slice: x: 4, y: 4 (y_hi: 2, y_lo: 2; y = y_hi * 2 + y_lo), z: 4, core: 2. Of those that a mesh axis runs over, the one named last changes fastest.
Arguments:
- flow_state: float32 [5, 256, 256, 128], P(None, 'sector', 'axial'), may hold values from -6 to 6
- damping: float32 [256, 256, 128], P('sector', 'axial'), may hold values from 0.05 to 0.5
- jacobians: float32 [3, 5, 5], replicated, may hold values from -2.5 to 2.5
- face_weight: float32 [5, 256, 256], P(None, 'sector', 'axial'), may hold values from -3 to 3
- phase_shift: int32 [4], replicated, may hold values from 0 to 255, as said below
- face_list: int32 [128, 128, 4], P(('sector', 'axial')), may hold values from 0 to 3, as said below
- face_count: int32 [128, 128], P(('sector', 'axial')), may hold values from 0 to 4, as said below
- arrival_bin: int32 [128, 128, 4, 2, 128], P(('sector', 'axial')), may hold values from 0 to 123
- arrival_fraction: float32 [128, 128, 4, 2, 128], P(('sector', 'axial')), may hold values from 0 to 1
- arrival_gain: float32 [128, 128, 4, 2, 128], P(('sector', 'axial')), may hold values from 0.005 to 0.05
Outputs:
- new_state: float32 [5, 256, 256, 128], P(None, 'sector', 'axial')
- signal: float32 [256, 128], P(('sector', 'axial'))
The draws below stay inside these ranges and needn't reach their ends.
Inputs may be any that keep to these rules, and one draw needn't show every extreme that they name: `phase_shift`: in one substep the offset lies between 128 and 143, in another it is 255, and in another 0. `face_list`: the entries of one list are distinct face blocks of the source device; entries at or past the count are padding. `face_count`: some observer owner has 4 live entries from every source device.
All inputs are finite; a program needn't handle non-finite values.
Results may differ from the reference program's by a relative error of at most 0.0003.
Values sent between devices are 32-bit elements; how exact they have to be, the bound alone decides.
A program may use at most 128 MiB of HBM per device.

```python
import math
import jax
import jax.numpy as jnp
from jax import lax

NV = 5
CT = 16
CZ = 32
NR = 128
SECTIONS = 4
FACE = 128
CAP = 4
OBS = 2
NBIN = 128
NT = 256
NZ = 256
FBD = 4
N_SECTOR = 16
N_AXIAL = 8


def draw_phase_shift(key, part):
    key = jax.random.fold_in(key, 13)
    first_key, second_key, third_key = jax.random.split(key, 3)
    shifts = jax.random.randint(first_key, (SECTIONS,), 0, NT)
    order = jax.random.permutation(second_key, SECTIONS)
    opposite = NT // 2 + jax.random.randint(third_key, (), 0, CT)
    shifts = jnp.where(jnp.arange(SECTIONS) == order[0], opposite, shifts)
    shifts = jnp.where(jnp.arange(SECTIONS) == order[1], NT - 1, shifts)
    shifts = jnp.where(jnp.arange(SECTIONS) == order[2], 0, shifts)
    return shifts.astype(jnp.int32)


def draw_face_list(key, part):
    key = jax.random.fold_in(key, 12)
    owners = N_SECTOR * N_AXIAL
    keys = jax.random.split(key, owners * owners)

    def one_order(single):
        return jax.random.permutation(single, FBD)
    orders = jax.vmap(one_order)(keys)
    return orders[:, :CAP].reshape(owners, owners, CAP).astype(jnp.int32)


def draw_face_count(key, part):
    key = jax.random.fold_in(key, 11)
    owners = N_SECTOR * N_AXIAL
    first_key, second_key, third_key = jax.random.split(key, 3)
    busy = jax.random.randint(first_key, (owners,), 0, 8) == 0
    favored = jax.random.randint(second_key, (), 0, owners)
    busy = busy | (jnp.arange(owners) == favored)
    sparse = jax.random.randint(third_key, (owners, owners), 0, CAP // 2 + 1)
    return jnp.where(busy[None, :], CAP, sparse).astype(jnp.int32)


def place_ends(drawn, stream_key, low, largest):
    longest = drawn.shape.index(max(drawn.shape))
    spots = []
    for shift in (0, 1):
        where = [jax.random.randint(jax.random.fold_in(stream_key, axis), (), 0, length) for axis, length in enumerate(drawn.shape)]
        where[longest] = (where[longest] + shift) % drawn.shape[longest]
        spots.append(tuple(where))
    return drawn.at[spots[0]].set(low).at[spots[1]].set(largest)


def steps_of(key, extent, pieces, low, largest):
    factor_of = 1.0
    for position, shards_of in pieces:
        draws = jax.random.uniform(jax.random.fold_in(jax.random.fold_in(key, 6), position), (shards_of,), jnp.float32, low / len(pieces), largest / len(pieces))
        factor_of = factor_of * jnp.repeat(jnp.exp(draws), extent[position] // shards_of).reshape((-1,) + (1,) * (len(extent) - 1 - position))
    return factor_of


def noise(key, shape, deviation, most, pieces=(), kind=jnp.bfloat16):
    drawn = deviation * jax.random.normal(key, shape, jnp.float32)
    if pieces:
        drawn = drawn * steps_of(key, shape, pieces, -0.22, 0.18)
    return jnp.clip(drawn, -most, most).astype(kind)


def setup_inputs(seed: int = 0) -> dict:
    splits = jax.random.split(jax.random.key(seed), 11)
    flow_state = noise(splits[0], (NV, NT, NZ, NR), 1.0, 6.0, ((1, 16), (2, 8)), jnp.float32)
    damping = jnp.clip(jnp.exp(math.log(0.5) - 2.3025851 * jax.random.uniform(splits[1], (NT, NZ, NR), jnp.float32) ** steps_of(splits[1], (NT, NZ, NR), ((0, 16), (1, 8)), -0.2, 0.2)), 0.05, 0.5)
    jacobians = noise(splits[2], (3, NV, NV), NV ** -0.5, 2.5, (), jnp.float32)
    face_weight = noise(splits[3], (NV, NT, NZ), 0.5, 3.0, ((1, 16), (2, 8)), jnp.float32)
    phase_shift = draw_phase_shift(jax.random.fold_in(splits[10], 71), 0)
    face_list = draw_face_list(jax.random.fold_in(splits[10], 71), 0)
    face_count = draw_face_count(jax.random.fold_in(splits[10], 71), 0)
    arrival_bin = place_ends(jax.random.randint(splits[7], (N_SECTOR * N_AXIAL, N_SECTOR * N_AXIAL, CAP, OBS, FACE), 0, NBIN - SECTIONS), jax.random.fold_in(splits[7], 1), 0, (NBIN - SECTIONS) - 1).astype(jnp.int32)
    arrival_fraction = jnp.clip(1.0 * jax.random.uniform(splits[8], (N_SECTOR * N_AXIAL, N_SECTOR * N_AXIAL, CAP, OBS, FACE), jnp.float32) ** steps_of(splits[8], (N_SECTOR * N_AXIAL, N_SECTOR * N_AXIAL, CAP, OBS, FACE), ((0, 128),), -0.2, 0.2), 0.0, 1.0)
    arrival_gain = jnp.clip(jnp.exp(math.log(0.05) - 2.3025851 * jax.random.uniform(splits[9], (N_SECTOR * N_AXIAL, N_SECTOR * N_AXIAL, CAP, OBS, FACE), jnp.float32) ** steps_of(splits[9], (N_SECTOR * N_AXIAL, N_SECTOR * N_AXIAL, CAP, OBS, FACE), ((0, 128),), -0.2, 0.2)), 0.005, 0.05)
    return dict(flow_state=flow_state, damping=damping, jacobians=jacobians, face_weight=face_weight, phase_shift=phase_shift, face_list=face_list, face_count=face_count, arrival_bin=arrival_bin, arrival_fraction=arrival_fraction, arrival_gain=arrival_gain)


time_step = 0.3
viscosity = 0.05


def apply_jacobian(matrix, flow_field):
    return jnp.einsum("ij,jtzr->itzr", matrix, flow_field, precision=lax.Precision.HIGHEST)


def tendency(flow_field, jacobians, damping, rotation):
    middle = NZ // 2
    theta_plus = jnp.roll(flow_field, -1, axis=1)
    theta_minus = jnp.roll(flow_field, 1, axis=1)
    zero_plane = jnp.zeros_like(flow_field[:, :, :1])
    axial_plus = jnp.concatenate([flow_field[:, :, 1:], zero_plane], axis=2)
    axial_minus = jnp.concatenate([zero_plane, flow_field[:, :, :-1]], axis=2)
    aft_ghost = jnp.roll(flow_field[:, :, middle - 1], rotation, axis=1)
    front_ghost = jnp.roll(flow_field[:, :, middle], -rotation, axis=1)
    axial_minus = axial_minus.at[:, :, middle].set(aft_ghost)
    axial_plus = axial_plus.at[:, :, middle - 1].set(front_ghost)
    zero_column = jnp.zeros_like(flow_field[..., :1])
    radial_plus = jnp.concatenate([flow_field[..., 1:], zero_column], axis=3)
    radial_minus = jnp.concatenate([zero_column, flow_field[..., :-1]], axis=3)
    advection = (apply_jacobian(jacobians[0], 0.5 * (theta_plus - theta_minus))
                 + apply_jacobian(jacobians[1], 0.5 * (axial_plus - axial_minus))
                 + apply_jacobian(jacobians[2], 0.5 * (radial_plus - radial_minus)))
    laplacian = theta_plus + theta_minus + axial_plus + axial_minus + radial_plus + radial_minus - 6.0 * flow_field
    return viscosity * laplacian - advection - damping[None] * flow_field


def surface_sources(flow_field, face_weight):
    surface = flow_field[:, :, :, NR // 2]
    values = jnp.sum(face_weight * surface, axis=0)
    blocks = values.reshape(N_SECTOR, CT, N_AXIAL, CZ).transpose(0, 2, 1, 3)
    return blocks.reshape(N_SECTOR * N_AXIAL, FBD, FACE)


def reference(flow_state, damping, jacobians, face_weight, phase_shift, face_list, face_count, arrival_bin, arrival_fraction, arrival_gain):
    rate_one = tendency(flow_state, jacobians, damping, phase_shift[0])
    section_two = flow_state + (0.5 * time_step) * rate_one
    rate_two = tendency(section_two, jacobians, damping, phase_shift[1])
    section_three = flow_state + (0.5 * time_step) * rate_two
    rate_three = tendency(section_three, jacobians, damping, phase_shift[2])
    section_four = flow_state + time_step * rate_three
    rate_four = tendency(section_four, jacobians, damping, phase_shift[3])
    new_state = flow_state + (time_step / 6.0) * (rate_one + 2.0 * rate_two + 2.0 * rate_three + rate_four)
    sources = jnp.stack([surface_sources(flow_state, face_weight), surface_sources(section_two, face_weight),
                         surface_sources(section_three, face_weight), surface_sources(section_four, face_weight)], axis=2)
    devices_all = N_SECTOR * N_AXIAL
    source_index = jnp.arange(devices_all, dtype=jnp.int32)[:, None]
    slot_index = jnp.arange(CAP, dtype=jnp.int32)[None, :]

    def owner_signal(inputs):
        block_lists, counts, bins, fractions, gains = inputs
        chosen = sources[source_index, block_lists.astype(jnp.int32)]
        live_slot = (slot_index < counts[:, None]).astype(jnp.float32)
        chosen = chosen * live_slot[:, :, None, None]
        observer_index = jnp.broadcast_to(jnp.arange(OBS, dtype=jnp.int32)[None, None, :, None], bins.shape)
        result = jnp.zeros((OBS, NBIN), jnp.float32)
        for sample in range(SECTIONS):
            amplitude = gains * chosen[:, :, sample][:, :, None, :]
            result = result.at[observer_index, bins + sample].add(amplitude * (1.0 - fractions))
            result = result.at[observer_index, bins + sample + 1].add(amplitude * fractions)
        return result

    signals = lax.map(owner_signal, (jnp.swapaxes(face_list, 0, 1), jnp.swapaxes(face_count, 0, 1),
                                     arrival_bin, arrival_fraction, arrival_gain))
    return new_state, signals.reshape(devices_all * OBS, NBIN)
```

```python
import jax
import jax.numpy as jnp
from jax import lax
from jax.experimental import pallas as pl
from jax.experimental.pallas import tpu as pltpu
from jax.sharding import PartitionSpec as P

NV = 5
NA = 16
NB = 8
CT = 16
CZ = 32
NR = 128
ROWS = CT * CZ
PAD = ROWS + 2 * CZ
NBIN = 128
PIECE = 8

time_step = 0.3
viscosity = 0.05

MESH = pl.DeviceIdType.MESH


def wait_rows(ref, sem):
    pltpu.make_async_copy(ref, ref, sem).wait()


def step_kernel(
    x_ref,
    damp_ref,
    jac_ref,
    fw_ref,
    shift_ref,
    list_ref,
    new_ref,
    gather_ref,
    s1,
    s2,
    s3,
    s4,
    edge_lo,
    edge_hi,
    ghost_lo,
    ghost_hi,
    row_out,
    row_sel,
    held1,
    held2,
    held3,
    held4,
    in1,
    in2,
    in3,
    in4,
    window,
    parcel,
    load_sem,
    theta_send,
    theta_recv,
    axial_send,
    axial_recv,
    row_send,
    row_recv,
    sel_send,
    sel_recv,
    ring_send,
    ring_recv,
    line_send,
    line_recv,
):
    a = lax.axis_index("sector")
    b = lax.axis_index("axial")
    front = b == NB // 2 - 1
    aft = b == NB // 2
    interface = jnp.logical_or(front, aft)
    other = jnp.where(front, NB // 2, NB // 2 - 1)
    has_lo = jnp.logical_and(b > 0, jnp.logical_not(aft))
    has_hi = jnp.logical_and(b < NB - 1, jnp.logical_not(front))
    states = [s1, s2, s3, s4]
    row_held = [held1, held2, held3, held4]
    row_in = [in1, in2, in3, in4]

    load = pltpu.make_async_copy(x_ref, s1.at[:, pl.ds(CZ, ROWS), :], load_sem.at[0])
    load.start()

    barrier = pltpu.get_barrier_semaphore()

    @pl.loop(1, NA)
    def _(step):
        pl.semaphore_signal(barrier, inc=1, device_id=(lax.rem(a + step, NA), b), device_id_type=MESH)

    @pl.loop(1, NB)
    def _(step):
        pl.semaphore_signal(barrier, inc=1, device_id=(a, lax.rem(b + step, NB)), device_id_type=MESH)

    @pl.when(interface)
    def _():
        @pl.loop(0, NA)
        def _(step):
            pl.semaphore_signal(barrier, inc=1, device_id=(step, other), device_id_type=MESH)

    row_out[...] = jnp.zeros_like(row_out)
    parcel[...] = jnp.zeros_like(parcel)
    for k in range(4):
        @pl.when(b == 0)
        def _():
            ghost_lo[k] = jnp.zeros((NV, CT, NR), jnp.float32)

        @pl.when(b == NB - 1)
        def _():
            ghost_hi[k] = jnp.zeros((NV, CT, NR), jnp.float32)

    pl.semaphore_wait(barrier, jnp.where(interface, NA - 1 + NB - 1 + NA, NA - 1 + NB - 1))

    def ring_start(which):
        slot = pl.multiple_of((b * NA + a) * PIECE, PIECE)
        gather_ref[which, pl.ds(slot, PIECE), :] = parcel[which]

        @pl.loop(1, NA)
        def _(step):
            pltpu.make_async_remote_copy(
                src_ref=parcel.at[which],
                dst_ref=gather_ref.at[which, pl.ds(slot, PIECE), :],
                send_sem=ring_send.at[which],
                recv_sem=ring_recv.at[which],
                device_id=(lax.rem(a + step, NA), b),
                device_id_type=MESH,
            ).start()

    def line_start(which):
        wait_rows(gather_ref.at[which, pl.ds(0, (NA - 1) * PIECE), :], ring_recv.at[which])
        slot = pl.multiple_of(b * NA * PIECE, NA * PIECE)

        @pl.loop(1, NB)
        def _(step):
            pltpu.make_async_remote_copy(
                src_ref=gather_ref.at[which, pl.ds(slot, NA * PIECE), :],
                dst_ref=gather_ref.at[which, pl.ds(slot, NA * PIECE), :],
                send_sem=line_send.at[which],
                recv_sem=line_recv.at[which],
                device_id=(a, lax.rem(b + step, NB)),
                device_id_type=MESH,
            ).start()

    def line_wait(which):
        wait_rows(gather_ref.at[which, pl.ds(0, (NB - 1) * NA * PIECE), :], line_recv.at[which])

    def theta_copies(k):
        state = states[k]
        down = pltpu.make_async_remote_copy(
            src_ref=state.at[:, pl.ds(CZ, CZ), :],
            dst_ref=state.at[:, pl.ds(CZ + ROWS, CZ), :],
            send_sem=theta_send.at[k, 0],
            recv_sem=theta_recv.at[k, 0],
            device_id=(lax.rem(a + NA - 1, NA), b),
            device_id_type=MESH,
        )
        up = pltpu.make_async_remote_copy(
            src_ref=state.at[:, pl.ds(ROWS, CZ), :],
            dst_ref=state.at[:, pl.ds(0, CZ), :],
            send_sem=theta_send.at[k, 1],
            recv_sem=theta_recv.at[k, 1],
            device_id=(lax.rem(a + 1, NA), b),
            device_id_type=MESH,
        )
        return down, up

    def axial_copies(k):
        down = pltpu.make_async_remote_copy(
            src_ref=edge_lo.at[k],
            dst_ref=ghost_hi.at[k],
            send_sem=axial_send.at[k, 0],
            recv_sem=axial_recv.at[k, 0],
            device_id=(a, jnp.maximum(b - 1, 0)),
            device_id_type=MESH,
        )
        up = pltpu.make_async_remote_copy(
            src_ref=edge_hi.at[k],
            dst_ref=ghost_lo.at[k],
            send_sem=axial_send.at[k, 1],
            recv_sem=axial_recv.at[k, 1],
            device_id=(a, jnp.minimum(b + 1, NB - 1)),
            device_id_type=MESH,
        )
        return down, up

    def send_edges(k):
        state = states[k]

        @pl.when(front)
        def _():
            for v in range(NV):
                row_out[k, pl.ds(v, CT, stride=PIECE), :] = state[v, pl.ds(CZ + CZ - 1, CT, stride=CZ), :]

        @pl.when(aft)
        def _():
            for v in range(NV):
                row_out[k, pl.ds(v, CT, stride=PIECE), :] = state[v, pl.ds(CZ, CT, stride=CZ), :]

        @pl.when(interface)
        def _():
            @pl.loop(0, CT)
            def _(t):
                pltpu.make_async_remote_copy(
                    src_ref=row_out.at[k, pl.ds(pl.multiple_of(t * PIECE, PIECE), PIECE), :],
                    dst_ref=row_held[k].at[a],
                    send_sem=row_send.at[k],
                    recv_sem=row_recv.at[k],
                    device_id=(t, other),
                    device_id_type=MESH,
                ).start()

        down, up = theta_copies(k)
        down.start()
        up.start()
        down, up = axial_copies(k)

        @pl.when(has_lo)
        def _():
            for v in range(NV):
                edge_lo[k, v] = state[v, pl.ds(CZ, CT, stride=CZ), :]
            down.start()

        @pl.when(has_hi)
        def _():
            for v in range(NV):
                edge_hi[k, v] = state[v, pl.ds(CZ + CZ - 1, CT, stride=CZ), :]
            up.start()

    def turn(k):
        r = shift_ref[k]
        return jnp.where(front, r, (CT * NA - r) & (CT * NA - 1))

    def relay(k):
        @pl.when(interface)
        def _():
            wait_rows(row_held[k], row_recv.at[k])
            first = (turn(k) - a + CT - 1) >> 4

            @pl.loop(0, NA)
            def _(d):
                row_sel[k, d] = row_held[k][(d + first) & (NA - 1)]

            @pl.loop(1, NA)
            def _(step):
                d = lax.rem(a + step, NA)
                pltpu.make_async_remote_copy(
                    src_ref=row_sel.at[k, d],
                    dst_ref=row_in[k].at[a],
                    send_sem=sel_send.at[k],
                    recv_sem=sel_recv.at[k],
                    device_id=(d, b),
                    device_id_type=MESH,
                ).start()
            row_in[k][a] = row_sel[k, a]

    def land(k):
        @pl.when(interface)
        def _():
            wait_rows(row_in[k].at[pl.ds(0, NA - 1)], sel_recv.at[k])
            r = turn(k)
            for t in range(CT):
                window[pl.ds(t * PIECE, PIECE), :] = row_in[k][(r + t) & (CT - 1)]

        @pl.when(front)
        def _():
            for v in range(NV):
                ghost_hi[k, v] = window[pl.ds(v, CT, stride=PIECE), :]

        @pl.when(aft)
        def _():
            for v in range(NV):
                ghost_lo[k, v] = window[pl.ds(v, CT, stride=PIECE), :]

        down, up = axial_copies(k)

        @pl.when(has_hi)
        def _():
            down.wait_recv()

        @pl.when(has_lo)
        def _():
            up.wait_recv()

    lane = lax.broadcasted_iota(jnp.int32, (CZ, NR), 1)
    line = lax.broadcasted_iota(jnp.int32, (CZ, NR), 0)

    def plane(k, t):
        state = states[k]
        base = pl.multiple_of(t * CZ, CZ)
        here = pl.ds(pl.multiple_of(base + CZ, CZ), CZ)
        center = [state[v, here, :] for v in range(NV)]
        advection = [None] * NV
        total = [None] * NV
        for d in range(3):
            for j in range(NV):
                c = center[j]
                if d == 0:
                    upper = state[j, pl.ds(pl.multiple_of(base + 2 * CZ, CZ), CZ), :]
                    lower = state[j, pl.ds(base, CZ), :]
                elif d == 1:
                    upper = jnp.where(line == CZ - 1, 0.0, pltpu.roll(c, CZ - 1, 0))
                    lower = jnp.where(line == 0, 0.0, pltpu.roll(c, 1, 0))
                else:
                    upper = jnp.where(lane == NR - 1, 0.0, pltpu.roll(c, NR - 1, 1))
                    lower = jnp.where(lane == 0, 0.0, pltpu.roll(c, 1, 1))
                both = upper + lower
                total[j] = both if d == 0 else total[j] + both
                slope = upper - lower
                for i in range(NV):
                    term = (0.5 * jac_ref[d, i, j]) * slope
                    advection[i] = term if advection[i] is None else advection[i] + term
        drag = damp_ref[pl.ds(base, CZ), :] + 6.0 * viscosity
        for i in range(NV):
            rate = viscosity * total[i] - advection[i] - drag * center[i]
            start = s1[i, here, :] if k else center[i]
            if k < 3:
                scale = time_step if k == 2 else 0.5 * time_step
                states[k + 1][i, here, :] = start + scale * rate
            else:
                mix = (s2[i, here, :] + 2.0 * s3[i, here, :] + center[i] - start) * (1.0 / 3.0)
                new_ref[i, pl.ds(base, CZ), :] = mix + (time_step / 6.0) * rate

    def correct(k):
        for side, ghost in ((0, ghost_lo), (1, ghost_hi)):
            sign = 0.5 if side == 0 else -0.5
            row = 0 if side == 0 else CZ - 1
            values = [ghost[k, j] for j in range(NV)]
            for i in range(NV):
                rate = viscosity * values[i]
                for j in range(NV):
                    rate = rate + (sign * jac_ref[1, i, j]) * values[j]
                if k < 3:
                    scale = time_step if k == 2 else 0.5 * time_step
                    where = pl.ds(CZ + row, CT, stride=CZ)
                    states[k + 1][i, where, :] = states[k + 1][i, where, :] + scale * rate
                else:
                    where = pl.ds(row, CT, stride=CZ)
                    new_ref[i, where, :] = new_ref[i, where, :] + (time_step / 6.0) * rate

    pick = (lax.broadcasted_iota(jnp.int32, (8, NR), 1) == NR // 2).astype(jnp.float32)

    def sample(k):
        state = states[k]
        total = None
        for v in range(NV):
            column = lax.dot_general(
                pick,
                state[v, pl.ds(CZ, ROWS), :],
                (((1,), (1,)), ((), ())),
                precision=lax.Precision.HIGHEST,
                preferred_element_type=jnp.float32,
            )
            term = column[0:1] * fw_ref[v]
            total = term if total is None else total + term
        for block in range(4):
            row = 2 * block + k % 2
            parcel[1 + k // 2, row : row + 1, :] = total[:, block * 128 : (block + 1) * 128]

    parcel[0] = list_ref[...]
    ring_start(0)
    load.wait()
    send_edges(0)
    for k in range(4):
        @pl.loop(1, CT // 2)
        def _(t):
            plane(k, t)

        relay(k)

        @pl.loop(CT // 2, CT - 1)
        def _(t):
            plane(k, t)

        if k == 0:
            sample(0)
            line_start(0)
        elif k == 1:
            sample(1)
            ring_start(1)
        elif k == 2:
            line_start(1)
            sample(2)
        else:
            line_start(2)
        down, up = theta_copies(k)
        down.wait_recv()
        up.wait_recv()

        @pl.loop(0, 2)
        def _(side):
            plane(k, side * (CT - 1))

        land(k)
        correct(k)
        if k < 3:
            send_edges(k + 1)
        if k == 2:
            sample(3)
            ring_start(2)

    for which in range(3):
        line_wait(which)
        wait_rows(gather_ref.at[which, pl.ds(0, (NA - 1) * PIECE), :], ring_send.at[which])
        wait_rows(gather_ref.at[which, pl.ds(0, (NB - 1) * NA * PIECE), :], line_send.at[which])
    for k in range(4):
        down, up = theta_copies(k)
        down.wait_send()
        up.wait_send()
        down, up = axial_copies(k)

        @pl.when(has_lo)
        def _():
            down.wait_send()

        @pl.when(has_hi)
        def _():
            up.wait_send()

        @pl.when(interface)
        def _():
            wait_rows(row_out.at[k], row_send.at[k])
            wait_rows(row_sel.at[k, pl.ds(0, NA - 1)], sel_send.at[k])


def step_call(x, damping, jacobians, face_weight, phase_shift, lists):
    vmem = pl.BlockSpec(memory_space=pltpu.VMEM)
    smem = pl.BlockSpec(memory_space=pltpu.SMEM)
    state = pltpu.VMEM((NV, PAD, NR), jnp.float32)
    edge = pltpu.VMEM((4, NV, CT, NR), jnp.float32)
    row = pltpu.VMEM((4, CT * PIECE, NR), jnp.float32)
    held = pltpu.VMEM((NA, PIECE, NR), jnp.float32)
    dma = pltpu.SemaphoreType.DMA
    return pl.pallas_call(
        step_kernel,
        out_shape=(
            jax.ShapeDtypeStruct((NV, ROWS, NR), jnp.float32),
            jax.ShapeDtypeStruct((3, NA * NB * PIECE, NR), jnp.float32),
        ),
        in_specs=[pl.BlockSpec(memory_space=pl.ANY), vmem, smem, vmem, smem, vmem],
        out_specs=(vmem, vmem),
        scratch_shapes=[state] * 4
        + [edge] * 4
        + [row, pltpu.VMEM((4, NA, PIECE, NR), jnp.float32)]
        + [held] * 8
        + [pltpu.VMEM((CT * PIECE, NR), jnp.float32), pltpu.VMEM((3, PIECE, NR), jnp.float32)]
        + [dma((1,)), dma((4, 2)), dma((4, 2)), dma((4, 2)), dma((4, 2))]
        + [dma((4,))] * 4
        + [dma((3,))] * 4,
        compiler_params=pltpu.CompilerParams(
            collective_id=0, has_side_effects=True, vmem_limit_bytes=40 << 20
        ),
        name="substeps",
    )(x, damping, jacobians, face_weight, phase_shift, lists)


def bin_kernel(list_ref, bin_ref, fraction_ref, gain_ref, early_ref, late_ref, out_ref, total):
    step = pl.program_id(0)

    @pl.when(step == 0)
    def _():
        total[...] = jnp.zeros_like(total)

    place = lax.broadcasted_iota(jnp.int32, (8, 128), 0)
    low = place < 4
    sample = place % 4
    sign = jnp.where(low, -1.0, 1.0).astype(jnp.float32)
    shift = jnp.where(low, 1.0, 0.0).astype(jnp.float32)
    fine = lax.broadcasted_iota(jnp.int32, (32, 128), 0).astype(jnp.float32).astype(jnp.bfloat16)
    zero = jnp.zeros((16, 128), jnp.bfloat16)

    def spread(ref, row):
        return jnp.broadcast_to(ref[row : row + 1], (8, 128))

    for a in range(NA):
        gain = gain_ref[a, 0]
        fraction = fraction_ref[a, 0]
        bins = bin_ref[a, 0]
        coarse_bin = (bins >> 5).astype(jnp.float32)
        fine_bin = (bins & 31).astype(jnp.float32)
        early = early_ref[0, 0, a]
        late = late_ref[0, 0, a]
        lists = list_ref[0, 0, a]
        blocks = []
        for block in range(4):
            later = jnp.where(sample == 2, spread(late, 2 * block), spread(late, 2 * block + 1))
            later = jnp.where(sample == 1, spread(early, 2 * block + 1), later)
            blocks.append(jnp.where(sample == 0, spread(early, 2 * block), later))
        count = spread(lists, 4)
        weights = [[], []]
        selectors = [[], []]
        for c in range(4):
            listed = spread(lists, c)
            received = jnp.zeros((8, 128), jnp.float32)
            for block in range(4):
                received = jnp.where(listed == block, blocks[block], received)
            received = jnp.where(count > c, received, 0.0)
            for o in range(2):
                row = 2 * c + o
                part = received * (spread(gain, row) * (spread(fraction, row) * sign + shift))
                head = part.astype(jnp.bfloat16).astype(jnp.float32)
                both = jnp.concatenate([head, part - head], 0).astype(jnp.bfloat16)
                coarse = jnp.broadcast_to(coarse_bin[row : row + 1], (16, 128)).astype(jnp.bfloat16)
                weights[o].append(
                    jnp.concatenate([jnp.where(coarse == jnp.bfloat16(q), both, zero) for q in range(4)], 0)
                )
                within = jnp.broadcast_to(fine_bin[row : row + 1], (32, 128)).astype(jnp.bfloat16)
                selectors[o].append(jnp.where(within == fine, jnp.bfloat16(1), jnp.bfloat16(0)))
        for o in range(2):
            total[o] += lax.dot_general(
                jnp.concatenate(weights[o], 1),
                jnp.concatenate(selectors[o], 1),
                (((1,), (1,)), ((), ())),
                preferred_element_type=jnp.float32,
            )

    @pl.when(step == pl.num_programs(0) - 1)
    def _():
        for o in range(2):
            signal = jnp.zeros((1, NBIN), jnp.float32)
            for q in range(8):
                offset = q % 4 + q // 4
                pieces = [
                    total[o, 16 * g + q : 16 * g + q + 1, :] + total[o, 16 * g + 8 + q : 16 * g + 9 + q, :]
                    for g in range(4)
                ]
                whole = jnp.concatenate(pieces, 1)
                signal = signal + (pltpu.roll(whole, offset, 1) if offset else whole)
            out_ref[o : o + 1, :] = signal


def bin_call(gathered, lists, bins, fractions, gains):
    owned = pl.BlockSpec((NA, 1, PIECE, 128), lambda s: (0, s, 0, 0))

    def part(which):
        return pl.BlockSpec((1, 1, NA, PIECE, 128), lambda s: (which, s, 0, 0, 0))

    return pl.pallas_call(
        bin_kernel,
        grid=(NB,),
        in_specs=[part(0), owned, owned, owned, part(1), part(2)],
        out_specs=pl.BlockSpec((2, NBIN), lambda s: (0, 0)),
        out_shape=jax.ShapeDtypeStruct((2, NBIN), jnp.float32),
        scratch_shapes=[pltpu.VMEM((2, 64, 32), jnp.float32)],
        compiler_params=pltpu.CompilerParams(vmem_limit_bytes=40 << 20),
        name="binning",
    )(lists, bins, fractions, gains, gathered, gathered)


def local(
    flow_state,
    damping,
    jacobians,
    face_weight,
    phase_shift,
    face_list,
    face_count,
    arrival_bin,
    arrival_fraction,
    arrival_gain,
):
    lists = jnp.concatenate(
        [face_list[0].T, face_count, jnp.zeros((3, NA * NB), jnp.int32)], axis=0
    ).astype(jnp.float32)
    new_state, gathered = step_call(
        flow_state.reshape(NV, ROWS, NR),
        damping.reshape(ROWS, NR),
        jacobians,
        face_weight.reshape(NV, 1, ROWS),
        phase_shift,
        lists,
    )
    owner = lax.axis_index("sector") * NB + lax.axis_index("axial")
    mine = lax.dynamic_slice_in_dim(gathered[0], owner, 1, axis=1)
    lists = jnp.broadcast_to(mine, (NA * NB * PIECE, NR)).reshape(1, NB, NA, PIECE, NR)
    signal = bin_call(
        gathered.reshape(3, NB, NA, PIECE, NR),
        lists,
        arrival_bin.reshape(NA, NB, PIECE, 128),
        arrival_fraction.reshape(NA, NB, PIECE, 128),
        arrival_gain.reshape(NA, NB, PIECE, 128),
    )
    return new_state.reshape(NV, CT, CZ, NR), signal


def solution(mesh):
    return jax.shard_map(
        local,
        mesh=mesh,
        in_specs=(
            P(None, "sector", "axial", None),
            P("sector", "axial", None),
            P(),
            P(None, "sector", "axial"),
            P(),
            P(("sector", "axial"), None, None),
            P(("sector", "axial"), None),
            P(("sector", "axial"), None, None, None, None),
            P(("sector", "axial"), None, None, None, None),
            P(("sector", "axial"), None, None, None, None),
        ),
        out_specs=(P(None, "sector", "axial", None), P(("sector", "axial"), None)),
        check_vma=False,
    )
```

```python
import functools

import jax
import jax.numpy as jnp
from jax import lax
from jax.experimental import pallas as pl
from jax.experimental.pallas import tpu as pltpu
from jax.sharding import PartitionSpec as P

NV = 5
NA = 16
NB = 8
CT = 16
CZ = 32
NR = 128
ROWS = CT * CZ
PAD = ROWS + 2 * CZ
NBIN = 128
PIECE = 8

time_step = 0.3
viscosity = 0.05

MESH = pl.DeviceIdType.MESH


def wait_rows(ref, sem):
    pltpu.make_async_copy(ref, ref, sem).wait()


def step_kernel(
    free,
    x_hbm,
    damp_hbm,
    jac_hbm,
    fw_hbm,
    shift_hbm,
    list_hbm,
    count_hbm,
    new_ref,
    lists_ref,
    early_ref,
    middle_ref,
    late_ref,
    damp_ref,
    jac_ref,
    fw_ref,
    shift_ref,
    list_ref,
    count_ref,
    weight,
    s1,
    s2,
    s3,
    s4,
    edge_lo,
    edge_hi,
    ghost_lo,
    ghost_hi,
    row_out,
    row_sel,
    held,
    incoming,
    near1,
    near2,
    near3,
    window,
    list_out,
    list_mid,
    list_stage,
    parcel0,
    parcel1,
    parcel2,
    load_sem,
    theta_send,
    theta_recv,
    axial_send,
    axial_recv,
    row_send,
    row_recv,
    sel_send,
    sel_recv,
    list_send,
    list_recv,
    ring_send,
    ring_recv,
    line_send,
    line_recv,
    pair_send,
    pair_recv,
):
    a = lax.axis_index("sector")
    b = lax.axis_index("axial")
    front = b == NB // 2 - 1
    aft = b == NB // 2
    interface = jnp.logical_or(front, aft)
    other = jnp.where(front, NB // 2, NB // 2 - 1)
    has_lo = jnp.logical_and(b > 0, jnp.logical_not(aft))
    has_hi = jnp.logical_and(b < NB - 1, jnp.logical_not(front))
    states = [s1, s2, s3, s4]
    direct = [k for k in range(4) if k != free]
    near = dict(zip(direct, (near1, near2, near3)))
    parcels = [parcel0, parcel1, parcel2]
    gathers = [early_ref, middle_ref, late_ref]

    loads = [
        pltpu.make_async_copy(source, target, load_sem.at[n])
        for n, (source, target) in enumerate(
            (
                (x_hbm, s1.at[:, pl.ds(CZ, ROWS), :]),
                (fw_hbm, fw_ref),
                (list_hbm, list_ref),
                (count_hbm, count_ref),
                (shift_hbm, shift_ref),
                (jac_hbm, jac_ref),
                (damp_hbm, damp_ref),
            )
        )
    ]
    for load in loads:
        load.start()

    barrier = pltpu.get_barrier_semaphore()

    @pl.loop(1, NA)
    def _(step):
        pl.semaphore_signal(barrier, inc=1, device_id=(lax.rem(a + step, NA), b), device_id_type=MESH)

    @pl.loop(1, NB)
    def _(step):
        pl.semaphore_signal(barrier, inc=1, device_id=(a, lax.rem(b + step, NB)), device_id_type=MESH)

    @pl.when(interface)
    def _():
        @pl.loop(0, NA)
        def _(step):
            pl.semaphore_signal(barrier, inc=1, device_id=(step, other), device_id_type=MESH)

    window[...] = jnp.zeros_like(window)
    weight[...] = jnp.zeros_like(weight)
    for k in range(4):
        @pl.when(b == 0)
        def _():
            ghost_lo[k] = jnp.zeros((NV, CT, NR), jnp.float32)

        @pl.when(b == NB - 1)
        def _():
            ghost_hi[k] = jnp.zeros((NV, CT, NR), jnp.float32)


    def list_rows(n):
        return pl.ds(pl.multiple_of(n * NB, NB), NB)

    def list_first():
        list_mid[list_rows(a), :] = list_out[list_rows(a), :]

        @pl.loop(1, NA)
        def _(step):
            to = lax.rem(a + step, NA)
            pltpu.make_async_remote_copy(
                src_ref=list_out.at[list_rows(to), :],
                dst_ref=list_mid.at[list_rows(a), :],
                send_sem=list_send.at[0],
                recv_sem=list_recv.at[0],
                device_id=(to, b),
                device_id_type=MESH,
            ).start()

    def list_second():
        wait_rows(list_mid.at[pl.ds(0, (NA - 1) * NB), :], list_recv.at[0])
        for n in range(NB):
            list_stage[n] = list_mid[pl.ds(n, NA, stride=NB), :]
        lists_ref[b] = list_stage[b]

        @pl.loop(1, NB)
        def _(step):
            to = lax.rem(b + step, NB)
            pltpu.make_async_remote_copy(
                src_ref=list_stage.at[to],
                dst_ref=lists_ref.at[b],
                send_sem=list_send.at[1],
                recv_sem=list_recv.at[1],
                device_id=(a, to),
                device_id_type=MESH,
            ).start()

    def list_wait():
        wait_rows(lists_ref.at[pl.ds(0, NB - 1)], list_recv.at[1])
        wait_rows(list_mid.at[pl.ds(0, (NA - 1) * NB), :], list_send.at[0])
        wait_rows(lists_ref.at[pl.ds(0, NB - 1)], list_send.at[1])

    core = lax.rem(a, 2)
    chip = a // 2

    def ring_start(which):
        gathers[which][b, core, chip] = parcels[which][...]

        @pl.loop(1, NA // 2)
        def _(step):
            pltpu.make_async_remote_copy(
                src_ref=parcels[which],
                dst_ref=gathers[which].at[b, core, chip],
                send_sem=ring_send.at[which],
                recv_sem=ring_recv.at[which],
                device_id=(lax.rem(a + 2 * step, NA), b),
                device_id_type=MESH,
            ).start()

    def line_start(which):
        wait_rows(gathers[which].at[0, 0, pl.ds(0, NA // 2 - 1)], ring_recv.at[which])

        @pl.loop(1, NB)
        def _(step):
            pltpu.make_async_remote_copy(
                src_ref=gathers[which].at[b, core],
                dst_ref=gathers[which].at[b, core],
                send_sem=line_send.at[which],
                recv_sem=line_recv.at[which],
                device_id=(a, lax.rem(b + step, NB)),
                device_id_type=MESH,
            ).start()

    def pair_copy(which):
        return pltpu.make_async_remote_copy(
            src_ref=gathers[which].at[:, core],
            dst_ref=gathers[which].at[:, core],
            send_sem=pair_send.at[which],
            recv_sem=pair_recv.at[which],
            device_id=(a + 1 - 2 * core, b),
            device_id_type=MESH,
        )

    def pair_start(which):
        wait_rows(gathers[which].at[pl.ds(0, NB - 1), 0], line_recv.at[which])
        pair_copy(which).start()

    def theta_copies(k):
        state = states[k]
        down = pltpu.make_async_remote_copy(
            src_ref=state.at[:, pl.ds(CZ, CZ), :],
            dst_ref=state.at[:, pl.ds(CZ + ROWS, CZ), :],
            send_sem=theta_send.at[k, 0],
            recv_sem=theta_recv.at[k, 0],
            device_id=(lax.rem(a + NA - 1, NA), b),
            device_id_type=MESH,
        )
        up = pltpu.make_async_remote_copy(
            src_ref=state.at[:, pl.ds(ROWS, CZ), :],
            dst_ref=state.at[:, pl.ds(0, CZ), :],
            send_sem=theta_send.at[k, 1],
            recv_sem=theta_recv.at[k, 1],
            device_id=(lax.rem(a + 1, NA), b),
            device_id_type=MESH,
        )
        return down, up

    def axial_copies(k):
        down = pltpu.make_async_remote_copy(
            src_ref=edge_lo.at[k],
            dst_ref=ghost_hi.at[k],
            send_sem=axial_send.at[k, 0],
            recv_sem=axial_recv.at[k, 0],
            device_id=(a, jnp.maximum(b - 1, 0)),
            device_id_type=MESH,
        )
        up = pltpu.make_async_remote_copy(
            src_ref=edge_hi.at[k],
            dst_ref=ghost_lo.at[k],
            send_sem=axial_send.at[k, 1],
            recv_sem=axial_recv.at[k, 1],
            device_id=(a, jnp.minimum(b + 1, NB - 1)),
            device_id_type=MESH,
        )
        return down, up

    def send_edges(k):
        state = states[k]

        @pl.when(front)
        def _():
            for v in range(NV):
                window[pl.ds(v, CT, stride=PIECE), :] = state[v, pl.ds(CZ + CZ - 1, CT, stride=CZ), :]

        @pl.when(aft)
        def _():
            for v in range(NV):
                window[pl.ds(v, CT, stride=PIECE), :] = state[v, pl.ds(CZ, CT, stride=CZ), :]

        @pl.when(interface)
        def _():
            for t in range(CT):
                row_out[k, t] = window[pl.ds(t * PIECE, PIECE), :]

            if k == free:
                @pl.loop(0, CT)
                def _(t):
                    pltpu.make_async_remote_copy(
                        src_ref=row_out.at[k, t],
                        dst_ref=held.at[a],
                        send_sem=row_send.at[k],
                        recv_sem=row_recv.at[k],
                        device_id=(t, other),
                        device_id_type=MESH,
                    ).start()
            else:
                for target, first, place, count in (
                    (a, 0, 8, 16),
                    (a + 8, 0, jnp.where(front, 48, 32), 16),
                    (a + jnp.where(front, 9, 7), 0, jnp.where(front, 32, 48), 16),
                    (a + jnp.where(front, NA - 1, 1), jnp.where(front, 0, 8), jnp.where(front, 24, 0), 8),
                ):
                    pltpu.make_async_remote_copy(
                        src_ref=row_out.at[k, pl.ds(first, count), pl.ds(0, NV), :],
                        dst_ref=near[k].at[pl.ds(place, count), pl.ds(0, NV), :],
                        send_sem=row_send.at[k],
                        recv_sem=row_recv.at[k],
                        device_id=(lax.rem(target, NA), other),
                        device_id_type=MESH,
                    ).start()

        down, up = theta_copies(k)
        down.start()
        up.start()
        down, up = axial_copies(k)

        @pl.when(has_lo)
        def _():
            for v in range(NV):
                edge_lo[k, v] = state[v, pl.ds(CZ, CT, stride=CZ), :]
            down.start()

        @pl.when(has_hi)
        def _():
            for v in range(NV):
                edge_hi[k, v] = state[v, pl.ds(CZ + CZ - 1, CT, stride=CZ), :]
            up.start()

    def turn(k):
        r = shift_ref[k]
        return jnp.where(front, r, (CT * NA - r) & (CT * NA - 1))

    def relay():
        @pl.when(interface)
        def _():
            wait_rows(held, row_recv.at[free])
            first = (turn(free) - a + CT - 1) >> 4

            @pl.loop(0, NA)
            def _(d):
                row_sel[d] = held[(d + first) & (NA - 1)]

            @pl.loop(1, NA)
            def _(step):
                d = lax.rem(a + step, NA)
                pltpu.make_async_remote_copy(
                    src_ref=row_sel.at[d],
                    dst_ref=incoming.at[a],
                    send_sem=sel_send.at[0],
                    recv_sem=sel_recv.at[0],
                    device_id=(d, b),
                    device_id_type=MESH,
                ).start()
            incoming[a] = row_sel[a]

    def land(k):
        @pl.when(interface)
        def _():
            if k == free:
                wait_rows(incoming.at[pl.ds(0, NA - 1)], sel_recv.at[0])
                r = turn(k)
                for t in range(CT):
                    window[pl.ds(t * PIECE, PIECE), :] = incoming[(r + t) & (CT - 1)]
            else:
                wait_rows(near[k].at[pl.ds(0, 56), pl.ds(0, NV), :], row_recv.at[k])
                r = shift_ref[k]
                ahead = jnp.where(r == 0, 8, jnp.where(r == 255, 7, r - 96))
                behind = jnp.where(r == 0, 8, jnp.where(r == 255, 9, 176 - r))
                first = jnp.where(front, ahead, behind)
                for t in range(CT):
                    window[pl.ds(t * PIECE, PIECE), :] = near[k][(first + t) & 63]

        @pl.when(front)
        def _():
            for v in range(NV):
                ghost_hi[k, v] = window[pl.ds(v, CT, stride=PIECE), :]

        @pl.when(aft)
        def _():
            for v in range(NV):
                ghost_lo[k, v] = window[pl.ds(v, CT, stride=PIECE), :]

        down, up = axial_copies(k)

        @pl.when(has_hi)
        def _():
            down.wait_recv()

        @pl.when(has_lo)
        def _():
            up.wait_recv()

    lane = lax.broadcasted_iota(jnp.int32, (CZ, NR), 1)
    line = lax.broadcasted_iota(jnp.int32, (CZ, NR), 0)

    def plane(k, t):
        state = states[k]
        base = pl.multiple_of(t * CZ, CZ)
        here = pl.ds(pl.multiple_of(base + CZ, CZ), CZ)
        center = [state[v, here, :] for v in range(NV)]
        advection = [None] * NV
        total = [None] * NV
        for d in range(3):
            for j in range(NV):
                c = center[j]
                if d == 0:
                    upper = state[j, pl.ds(pl.multiple_of(base + 2 * CZ, CZ), CZ), :]
                    lower = state[j, pl.ds(base, CZ), :]
                elif d == 1:
                    upper = jnp.where(line == CZ - 1, 0.0, pltpu.roll(c, CZ - 1, 0))
                    lower = jnp.where(line == 0, 0.0, pltpu.roll(c, 1, 0))
                else:
                    upper = jnp.where(lane == NR - 1, 0.0, pltpu.roll(c, NR - 1, 1))
                    lower = jnp.where(lane == 0, 0.0, pltpu.roll(c, 1, 1))
                both = upper + lower
                total[j] = both if d == 0 else total[j] + both
                slope = upper - lower
                for i in range(NV):
                    term = (0.5 * jac_ref[i, d, j]) * slope
                    advection[i] = term if advection[i] is None else advection[i] + term
        drag = damp_ref[pl.ds(base, CZ), :] + 6.0 * viscosity
        for i in range(NV):
            rate = viscosity * total[i] - advection[i] - drag * center[i]
            start = s1[i, here, :] if k else center[i]
            if k < 3:
                scale = time_step if k == 2 else 0.5 * time_step
                states[k + 1][i, here, :] = start + scale * rate
            else:
                mix = (s2[i, here, :] + 2.0 * s3[i, here, :] + center[i] - start) * (1.0 / 3.0)
                new_ref[i, pl.ds(base, CZ), :] = mix + (time_step / 6.0) * rate

    def correct(k):
        for side, ghost in ((0, ghost_lo), (1, ghost_hi)):
            sign = 0.5 if side == 0 else -0.5
            row = 0 if side == 0 else CZ - 1
            values = [ghost[k, j] for j in range(NV)]
            for i in range(NV):
                rate = viscosity * values[i]
                for j in range(NV):
                    rate = rate + (sign * jac_ref[i, 1, j]) * values[j]
                if k < 3:
                    scale = time_step if k == 2 else 0.5 * time_step
                    where = pl.ds(CZ + row, CT, stride=CZ)
                    states[k + 1][i, where, :] = states[k + 1][i, where, :] + scale * rate
                else:
                    where = pl.ds(row, CT, stride=CZ)
                    new_ref[i, where, :] = new_ref[i, where, :] + (time_step / 6.0) * rate

    pick = (lax.broadcasted_iota(jnp.int32, (8, NR), 1) == NR // 2).astype(jnp.float32)

    def sample(k):
        state = states[k]
        total = None
        for v in range(NV):
            column = lax.dot_general(
                pick,
                state[v, pl.ds(CZ, ROWS), :],
                (((1,), (1,)), ((), ())),
                precision=lax.Precision.HIGHEST,
                preferred_element_type=jnp.float32,
            )
            term = column[0:1] * weight[v : v + 1, :]
            total = term if total is None else total + term
        for block in range(4):
            part = total[:, block * 128 : (block + 1) * 128]
            if k == 3:
                parcel2[block : block + 1, :] = part
            elif k == 2:
                parcel1[block : block + 1, :] = part
            else:
                parcel0[2 * block + k : 2 * block + k + 1, :] = part

    for load in loads:
        load.wait()
    for t in range(CT):
        weight[0:NV, t * CZ : (t + 1) * CZ] = fw_ref[:, t, :]
    rows = jnp.concatenate([list_ref[...], count_ref[...], jnp.zeros((3, NR), jnp.int32)], 0).astype(jnp.float32)
    places = lax.broadcasted_iota(jnp.int32, (8, NR), 0) == lax.broadcasted_iota(jnp.int32, (8, NR), 1)
    list_out[...] = lax.dot_general(
        rows,
        places.astype(jnp.float32),
        (((0,), (0,)), ((), ())),
        precision=lax.Precision.HIGHEST,
        preferred_element_type=jnp.float32,
    )
    sample(0)
    pl.semaphore_wait(barrier, jnp.where(interface, NA - 1 + NB - 1 + NA, NA - 1 + NB - 1))
    send_edges(0)
    list_first()
    for k in range(4):
        @pl.loop(1, CT // 2)
        def _(t):
            plane(k, t)

        if k == free:
            relay()

        @pl.loop(CT // 2, CT - 1)
        def _(t):
            plane(k, t)

        if k == 3:
            line_start(2)
            pair_start(1)
        down, up = theta_copies(k)
        down.wait_recv()
        up.wait_recv()

        @pl.loop(0, 2)
        def _(side):
            plane(k, side * (CT - 1))

        land(k)
        correct(k)
        if k < 3:
            send_edges(k + 1)
        if k == 0:
            sample(1)
            ring_start(0)
            list_second()
        elif k == 1:
            sample(2)
            ring_start(1)
            line_start(0)
        elif k == 2:
            sample(3)
            ring_start(2)
            line_start(1)
            pair_start(0)

    pair_start(2)
    list_wait()
    for which in range(3):
        wait_rows(gathers[which].at[0, 0, pl.ds(0, NA // 2 - 1)], ring_send.at[which])
        wait_rows(gathers[which].at[pl.ds(0, NB - 1), 0], line_send.at[which])
        pair_copy(which).wait()
    for k in range(4):
        down, up = theta_copies(k)
        down.wait_send()
        up.wait_send()
        down, up = axial_copies(k)

        @pl.when(has_lo)
        def _():
            down.wait_send()

        @pl.when(has_hi)
        def _():
            up.wait_send()

        @pl.when(interface)
        def _():
            if k == free:
                wait_rows(row_out.at[k], row_send.at[k])
                wait_rows(row_sel.at[pl.ds(0, NA - 1)], sel_send.at[0])
            else:
                wait_rows(near[k].at[pl.ds(0, 56), pl.ds(0, NV), :], row_send.at[k])


def step_call(free, x, damping, jacobians, face_weight, phase_shift, lists, counts):
    vmem = pl.BlockSpec(memory_space=pltpu.VMEM)
    hbm = pl.BlockSpec(memory_space=pltpu.HBM)
    state = pltpu.VMEM((NV, PAD, NR), jnp.float32)
    edge = pltpu.VMEM((4, NV, CT, NR), jnp.float32)
    row = pltpu.VMEM((NA, PIECE, NR), jnp.float32)
    dma = pltpu.SemaphoreType.DMA
    return pl.pallas_call(
        functools.partial(step_kernel, free),
        out_shape=(
            jax.ShapeDtypeStruct((NV, ROWS, NR), jnp.float32),
            jax.ShapeDtypeStruct((NB, NA, NR), jnp.float32),
            jax.ShapeDtypeStruct((NB, 2, NA // 2, 8, NR), jnp.float32),
            jax.ShapeDtypeStruct((NB, 2, NA // 2, 4, NR), jnp.float32),
            jax.ShapeDtypeStruct((NB, 2, NA // 2, 4, NR), jnp.float32),
        ),
        in_specs=[hbm] * 7,
        out_specs=(vmem,) * 5,
        scratch_shapes=[
            pltpu.VMEM((ROWS, NR), jnp.float32),
            pltpu.SMEM((NV, 3, NV), jnp.float32),
            pltpu.VMEM((NV, CT, CZ), jnp.float32),
            pltpu.SMEM((4,), jnp.int32),
            pltpu.VMEM((4, NR), jnp.int32),
            pltpu.VMEM((1, NR), jnp.int32),
            pltpu.VMEM((8, ROWS), jnp.float32),
        ]
        + [state] * 4
        + [edge] * 4
        + [pltpu.VMEM((4, CT, PIECE, NR), jnp.float32), row, row, row]
        + [pltpu.VMEM((64, PIECE, NR), jnp.float32)] * 3
        + [pltpu.VMEM((CT * PIECE, NR), jnp.float32)]
        + [pltpu.VMEM((NA * NB, NR), jnp.float32)] * 2
        + [pltpu.VMEM((NB, NA, NR), jnp.float32)]
        + [pltpu.VMEM((rows, NR), jnp.float32) for rows in (8, 4, 4)]
        + [dma((7,)), dma((4, 2)), dma((4, 2)), dma((4, 2)), dma((4, 2))]
        + [dma((4,)), dma((4,)), dma((1,)), dma((1,))]
        + [dma((2,))] * 2
        + [dma((3,))] * 6,
        compiler_params=pltpu.CompilerParams(
            collective_id=free, has_side_effects=True, vmem_limit_bytes=24 << 20
        ),
        name="substeps%d" % free,
    )(x, damping, jacobians, face_weight, phase_shift, lists, counts)


def bin_kernel(
    list_ref, bin_ref, fraction_ref, gain_ref, early_ref, middle_ref, late_ref, state_ref, out_ref, new_ref, total
):
    step = pl.program_id(0)
    new_ref[...] = state_ref[...]

    @pl.when(step == 0)
    def _():
        total[...] = jnp.zeros_like(total)

    place = lax.broadcasted_iota(jnp.int32, (8, 128), 0)
    low = place < 4
    sample = place % 4
    sign = jnp.where(low, -1.0, 1.0).astype(jnp.float32)
    shift = jnp.where(low, 1.0, 0.0).astype(jnp.float32)
    fine = lax.broadcasted_iota(jnp.int32, (32, 128), 0).astype(jnp.float32).astype(jnp.bfloat16)
    zero = jnp.zeros((16, 128), jnp.bfloat16)

    def spread(ref, row):
        return jnp.broadcast_to(ref[row : row + 1], (8, 128))

    spot = lax.broadcasted_iota(jnp.int32, (128, 5 * 128), 0)
    part_of = lax.broadcasted_iota(jnp.int32, (128, 5 * 128), 1) // 128
    wide = jnp.dot(
        list_ref[0].astype(jnp.bfloat16),
        (spot == part_of).astype(jnp.bfloat16),
        preferred_element_type=jnp.float32,
    )

    def entry(a, c):
        return jnp.broadcast_to(wide[a : a + 1, c * 128 : (c + 1) * 128], (8, 128))

    for a in range(NA):
        gain = gain_ref[a, 0]
        fraction = fraction_ref[a, 0]
        bins = bin_ref[a, 0]
        coarse_bin = (bins >> 5).astype(jnp.float32)
        fine_bin = (bins & 31).astype(jnp.float32)
        early = early_ref[0, a % 2, a // 2]
        middle = middle_ref[0, a % 2, a // 2]
        late = late_ref[0, a % 2, a // 2]
        blocks = []
        for block in range(4):
            later = jnp.where(sample == 2, spread(middle, block), spread(late, block))
            later = jnp.where(sample == 1, spread(early, 2 * block + 1), later)
            blocks.append(jnp.where(sample == 0, spread(early, 2 * block), later))
        count = entry(a, 4)
        weights = [[], []]
        selectors = [[], []]
        for c in range(4):
            listed = entry(a, c)
            received = jnp.zeros((8, 128), jnp.float32)
            for block in range(4):
                received = jnp.where(listed == block, blocks[block], received)
            received = jnp.where(count > c, received, 0.0)
            for o in range(2):
                row = 2 * c + o
                part = received * (spread(gain, row) * (spread(fraction, row) * sign + shift))
                head = part.astype(jnp.bfloat16).astype(jnp.float32)
                both = jnp.concatenate([head, part - head], 0).astype(jnp.bfloat16)
                coarse = jnp.broadcast_to(coarse_bin[row : row + 1], (16, 128)).astype(jnp.bfloat16)
                weights[o].append(
                    jnp.concatenate([jnp.where(coarse == jnp.bfloat16(q), both, zero) for q in range(4)], 0)
                )
                within = jnp.broadcast_to(fine_bin[row : row + 1], (32, 128)).astype(jnp.bfloat16)
                selectors[o].append(jnp.where(within == fine, jnp.bfloat16(1), jnp.bfloat16(0)))
        for o in range(2):
            total[o] += lax.dot_general(
                jnp.concatenate(weights[o], 1),
                jnp.concatenate(selectors[o], 1),
                (((1,), (1,)), ((), ())),
                preferred_element_type=jnp.float32,
            )

    @pl.when(step == pl.num_programs(0) - 1)
    def _():
        for o in range(2):
            signal = jnp.zeros((1, NBIN), jnp.float32)
            for q in range(8):
                offset = q % 4 + q // 4
                pieces = [
                    total[o, 16 * g + q : 16 * g + q + 1, :] + total[o, 16 * g + 8 + q : 16 * g + 9 + q, :]
                    for g in range(4)
                ]
                whole = jnp.concatenate(pieces, 1)
                signal = signal + (pltpu.roll(whole, offset, 1) if offset else whole)
            out_ref[o : o + 1, :] = signal


def bin_call(lists, bins, fractions, gains, early, middle, late, state):
    owned = pl.BlockSpec((NA, 1, PIECE, 128), lambda s: (0, s, 0, 0))

    def part(rows):
        return pl.BlockSpec((1, 2, NA // 2, rows, 128), lambda s: (s, 0, 0, 0, 0))

    slab = pl.BlockSpec((NV, ROWS // NB, NR), lambda s: (0, s, 0))
    return pl.pallas_call(
        bin_kernel,
        grid=(NB,),
        in_specs=[
            pl.BlockSpec((1, NA, 128), lambda s: (s, 0, 0)),
            owned,
            owned,
            owned,
            part(8),
            part(4),
            part(4),
            slab,
        ],
        out_specs=(pl.BlockSpec((2, NBIN), lambda s: (0, 0)), slab),
        out_shape=(
            jax.ShapeDtypeStruct((2, NBIN), jnp.float32),
            jax.ShapeDtypeStruct((NV, ROWS, NR), jnp.float32),
        ),
        scratch_shapes=[pltpu.VMEM((2, 64, 32), jnp.float32)],
        compiler_params=pltpu.CompilerParams(vmem_limit_bytes=24 << 20),
        name="binning",
    )(lists, bins, fractions, gains, early, middle, late, state)


def local(
    flow_state,
    damping,
    jacobians,
    face_weight,
    phase_shift,
    face_list,
    face_count,
    arrival_bin,
    arrival_fraction,
    arrival_gain,
):
    zero = phase_shift == 0
    last = phase_shift == CT * NA - 1
    opposite = jnp.logical_and(phase_shift >= 128, phase_shift < 144)
    apart = jnp.logical_not(jnp.eye(4, dtype=bool))

    def elsewhere(flags):
        return jnp.any(jnp.logical_and(apart, flags[None, :]), axis=1)

    rest = elsewhere(zero) & elsewhere(last) & elsewhere(opposite)
    free = jnp.min(jnp.where(rest, jnp.arange(4, dtype=jnp.int32), 3))
    state, lists, early, middle, late = lax.switch(
        free,
        [functools.partial(step_call, k) for k in range(4)],
        flow_state.reshape(NV, ROWS, NR),
        damping.reshape(ROWS, NR),
        jnp.transpose(jacobians, (1, 0, 2)),
        face_weight,
        phase_shift,
        face_list[0].T,
        face_count,
    )
    signal, new_state = bin_call(
        lists,
        arrival_bin.reshape(NA, NB, PIECE, 128),
        arrival_fraction.reshape(NA, NB, PIECE, 128),
        arrival_gain.reshape(NA, NB, PIECE, 128),
        early,
        middle,
        late,
        state,
    )
    return new_state.reshape(NV, CT, CZ, NR), signal


def solution(mesh):
    return jax.shard_map(
        local,
        mesh=mesh,
        in_specs=(
            P(None, "sector", "axial", None),
            P("sector", "axial", None),
            P(),
            P(None, "sector", "axial"),
            P(),
            P(("sector", "axial"), None, None),
            P(("sector", "axial"), None),
            P(("sector", "axial"), None, None, None, None),
            P(("sector", "axial"), None, None, None, None),
            P(("sector", "axial"), None, None, None, None),
        ),
        out_specs=(P(None, "sector", "axial", None), P(("sector", "axial"), None)),
        check_vma=False,
    )
```

```python
import functools

import jax
import jax.numpy as jnp
from jax import lax
from jax.experimental import pallas as pl
from jax.experimental.pallas import tpu as pltpu
from jax.sharding import PartitionSpec as P

NV = 5
NA = 16
NB = 8
CT = 16
CZ = 32
NR = 128
ROWS = CT * CZ
PAD = ROWS + 2 * CZ
NBIN = 128
PIECE = 8

time_step = 0.3
viscosity = 0.05

MESH = pl.DeviceIdType.MESH


def wait_rows(ref, sem):
    pltpu.make_async_copy(ref, ref, sem).wait()


def step_kernel(
    free,
    x_hbm,
    damp_hbm,
    jac_hbm,
    fw_hbm,
    shift_hbm,
    list_hbm,
    count_hbm,
    bin_hbm,
    fraction_hbm,
    gain_hbm,
    new_ref,
    signal_ref,
    lists_ref,
    early_ref,
    middle_ref,
    late_ref,
    bin_ref,
    fraction_ref,
    gain_ref,
    selector_ref,
    wide_ref,
    total,
    last_total,
    damp_ref,
    jac_ref,
    fw_ref,
    shift_ref,
    list_ref,
    count_ref,
    weight,
    s1,
    s2,
    s3,
    s4,
    edge_lo,
    edge_hi,
    ghost_lo,
    ghost_hi,
    row_out,
    row_sel,
    held,
    incoming,
    near1,
    near2,
    near3,
    window,
    list_out,
    list_mid,
    list_stage,
    parcel0,
    parcel1,
    parcel2,
    load_sem,
    theta_send,
    theta_recv,
    axial_send,
    axial_recv,
    row_send,
    row_recv,
    sel_send,
    sel_recv,
    list_send,
    list_recv,
    ring_send,
    ring_recv,
    line_send,
    line_recv,
    pair_send,
    pair_recv,
):
    a = lax.axis_index("sector")
    b = lax.axis_index("axial")
    front = b == NB // 2 - 1
    aft = b == NB // 2
    interface = jnp.logical_or(front, aft)
    other = jnp.where(front, NB // 2, NB // 2 - 1)
    has_lo = jnp.logical_and(b > 0, jnp.logical_not(aft))
    has_hi = jnp.logical_and(b < NB - 1, jnp.logical_not(front))
    states = [s1, s2, s3, s4]
    direct = [k for k in range(4) if k != free]
    near = dict(zip(direct, (near1, near2, near3)))
    parcels = [parcel0, parcel1, parcel2]
    gathers = [early_ref, middle_ref, late_ref]

    loads = [
        pltpu.make_async_copy(source, target, load_sem.at[n])
        for n, (source, target) in enumerate(
            (
                (x_hbm, s1.at[:, pl.ds(CZ, ROWS), :]),
                (fw_hbm, fw_ref),
                (list_hbm, list_ref),
                (count_hbm, count_ref),
                (shift_hbm, shift_ref),
                (jac_hbm, jac_ref),
                (damp_hbm, damp_ref),
                (bin_hbm, bin_ref),
                (fraction_hbm, fraction_ref),
                (gain_hbm, gain_ref),
            )
        )
    ]
    for load in loads:
        load.start()

    barrier = pltpu.get_barrier_semaphore()

    @pl.loop(1, NA)
    def _(step):
        pl.semaphore_signal(barrier, inc=1, device_id=(lax.rem(a + step, NA), b), device_id_type=MESH)

    @pl.loop(1, NB)
    def _(step):
        pl.semaphore_signal(barrier, inc=1, device_id=(a, lax.rem(b + step, NB)), device_id_type=MESH)

    @pl.when(interface)
    def _():
        @pl.loop(0, NA)
        def _(step):
            pl.semaphore_signal(barrier, inc=1, device_id=(step, other), device_id_type=MESH)

    window[...] = jnp.zeros_like(window)
    weight[...] = jnp.zeros_like(weight)
    for k in range(4):
        @pl.when(b == 0)
        def _():
            ghost_lo[k] = jnp.zeros((NV, CT, NR), jnp.float32)

        @pl.when(b == NB - 1)
        def _():
            ghost_hi[k] = jnp.zeros((NV, CT, NR), jnp.float32)


    def list_rows(n):
        return pl.ds(pl.multiple_of(n * NB, NB), NB)

    def list_first():
        list_mid[list_rows(a), :] = list_out[list_rows(a), :]

        @pl.loop(1, NA)
        def _(step):
            to = lax.rem(a + step, NA)
            pltpu.make_async_remote_copy(
                src_ref=list_out.at[list_rows(to), :],
                dst_ref=list_mid.at[list_rows(a), :],
                send_sem=list_send.at[0],
                recv_sem=list_recv.at[0],
                device_id=(to, b),
                device_id_type=MESH,
            ).start()

    def list_second():
        wait_rows(list_mid.at[pl.ds(0, (NA - 1) * NB), :], list_recv.at[0])
        for n in range(NB):
            list_stage[n] = list_mid[pl.ds(n, NA, stride=NB), :]
        lists_ref[b] = list_stage[b]

        @pl.loop(1, NB)
        def _(step):
            to = lax.rem(b + step, NB)
            pltpu.make_async_remote_copy(
                src_ref=list_stage.at[to],
                dst_ref=lists_ref.at[b],
                send_sem=list_send.at[1],
                recv_sem=list_recv.at[1],
                device_id=(a, to),
                device_id_type=MESH,
            ).start()

    def list_wait():
        wait_rows(lists_ref.at[pl.ds(0, NB - 1)], list_recv.at[1])
        wait_rows(list_mid.at[pl.ds(0, (NA - 1) * NB), :], list_send.at[0])
        wait_rows(lists_ref.at[pl.ds(0, NB - 1)], list_send.at[1])

    core = lax.rem(a, 2)
    chip = a // 2

    def ring_start(which):
        gathers[which][b, core, chip] = parcels[which][...]

        @pl.loop(1, NA // 2)
        def _(step):
            pltpu.make_async_remote_copy(
                src_ref=parcels[which],
                dst_ref=gathers[which].at[b, core, chip],
                send_sem=ring_send.at[which],
                recv_sem=ring_recv.at[which],
                device_id=(lax.rem(a + 2 * step, NA), b),
                device_id_type=MESH,
            ).start()

    def line_start(which):
        wait_rows(gathers[which].at[0, 0, pl.ds(0, NA // 2 - 1)], ring_recv.at[which])

        @pl.loop(1, NB)
        def _(step):
            pltpu.make_async_remote_copy(
                src_ref=gathers[which].at[b, core],
                dst_ref=gathers[which].at[b, core],
                send_sem=line_send.at[which],
                recv_sem=line_recv.at[which],
                device_id=(a, lax.rem(b + step, NB)),
                device_id_type=MESH,
            ).start()

    def pair_copy(which):
        return pltpu.make_async_remote_copy(
            src_ref=gathers[which].at[:, core],
            dst_ref=gathers[which].at[:, core],
            send_sem=pair_send.at[which],
            recv_sem=pair_recv.at[which],
            device_id=(a + 1 - 2 * core, b),
            device_id_type=MESH,
        )

    def pair_start(which):
        wait_rows(gathers[which].at[pl.ds(0, NB - 1), 0], line_recv.at[which])
        pair_copy(which).start()

    def theta_copies(k):
        state = states[k]
        down = pltpu.make_async_remote_copy(
            src_ref=state.at[:, pl.ds(CZ, CZ), :],
            dst_ref=state.at[:, pl.ds(CZ + ROWS, CZ), :],
            send_sem=theta_send.at[k, 0],
            recv_sem=theta_recv.at[k, 0],
            device_id=(lax.rem(a + NA - 1, NA), b),
            device_id_type=MESH,
        )
        up = pltpu.make_async_remote_copy(
            src_ref=state.at[:, pl.ds(ROWS, CZ), :],
            dst_ref=state.at[:, pl.ds(0, CZ), :],
            send_sem=theta_send.at[k, 1],
            recv_sem=theta_recv.at[k, 1],
            device_id=(lax.rem(a + 1, NA), b),
            device_id_type=MESH,
        )
        return down, up

    def axial_copies(k):
        down = pltpu.make_async_remote_copy(
            src_ref=edge_lo.at[k],
            dst_ref=ghost_hi.at[k],
            send_sem=axial_send.at[k, 0],
            recv_sem=axial_recv.at[k, 0],
            device_id=(a, jnp.maximum(b - 1, 0)),
            device_id_type=MESH,
        )
        up = pltpu.make_async_remote_copy(
            src_ref=edge_hi.at[k],
            dst_ref=ghost_lo.at[k],
            send_sem=axial_send.at[k, 1],
            recv_sem=axial_recv.at[k, 1],
            device_id=(a, jnp.minimum(b + 1, NB - 1)),
            device_id_type=MESH,
        )
        return down, up

    def send_edges(k):
        state = states[k]

        @pl.when(front)
        def _():
            for v in range(NV):
                window[pl.ds(v, CT, stride=PIECE), :] = state[v, pl.ds(CZ + CZ - 1, CT, stride=CZ), :]

        @pl.when(aft)
        def _():
            for v in range(NV):
                window[pl.ds(v, CT, stride=PIECE), :] = state[v, pl.ds(CZ, CT, stride=CZ), :]

        @pl.when(interface)
        def _():
            for t in range(CT):
                row_out[k, t] = window[pl.ds(t * PIECE, PIECE), :]

            if k == free:
                @pl.loop(0, CT)
                def _(t):
                    pltpu.make_async_remote_copy(
                        src_ref=row_out.at[k, t],
                        dst_ref=held.at[a],
                        send_sem=row_send.at[k],
                        recv_sem=row_recv.at[k],
                        device_id=(t, other),
                        device_id_type=MESH,
                    ).start()
            else:
                for target, first, place, count in (
                    (a, 0, 8, 16),
                    (a + 8, 0, jnp.where(front, 48, 32), 16),
                    (a + jnp.where(front, 9, 7), 0, jnp.where(front, 32, 48), 16),
                    (a + jnp.where(front, NA - 1, 1), jnp.where(front, 0, 8), jnp.where(front, 24, 0), 8),
                ):
                    pltpu.make_async_remote_copy(
                        src_ref=row_out.at[k, pl.ds(first, count), pl.ds(0, NV), :],
                        dst_ref=near[k].at[pl.ds(place, count), pl.ds(0, NV), :],
                        send_sem=row_send.at[k],
                        recv_sem=row_recv.at[k],
                        device_id=(lax.rem(target, NA), other),
                        device_id_type=MESH,
                    ).start()

        down, up = theta_copies(k)
        down.start()
        up.start()
        down, up = axial_copies(k)

        @pl.when(has_lo)
        def _():
            for v in range(NV):
                edge_lo[k, v] = state[v, pl.ds(CZ, CT, stride=CZ), :]
            down.start()

        @pl.when(has_hi)
        def _():
            for v in range(NV):
                edge_hi[k, v] = state[v, pl.ds(CZ + CZ - 1, CT, stride=CZ), :]
            up.start()

    def turn(k):
        r = shift_ref[k]
        return jnp.where(front, r, (CT * NA - r) & (CT * NA - 1))

    def relay():
        @pl.when(interface)
        def _():
            wait_rows(held, row_recv.at[free])
            first = (turn(free) - a + CT - 1) >> 4

            @pl.loop(0, NA)
            def _(d):
                row_sel[d] = held[(d + first) & (NA - 1)]

            @pl.loop(1, NA)
            def _(step):
                d = lax.rem(a + step, NA)
                pltpu.make_async_remote_copy(
                    src_ref=row_sel.at[d],
                    dst_ref=incoming.at[a],
                    send_sem=sel_send.at[0],
                    recv_sem=sel_recv.at[0],
                    device_id=(d, b),
                    device_id_type=MESH,
                ).start()
            incoming[a] = row_sel[a]

    def land(k):
        @pl.when(interface)
        def _():
            if k == free:
                wait_rows(incoming.at[pl.ds(0, NA - 1)], sel_recv.at[0])
                r = turn(k)
                for t in range(CT):
                    window[pl.ds(t * PIECE, PIECE), :] = incoming[(r + t) & (CT - 1)]
            else:
                wait_rows(near[k].at[pl.ds(0, 56), pl.ds(0, NV), :], row_recv.at[k])
                r = shift_ref[k]
                ahead = jnp.where(r == 0, 8, jnp.where(r == 255, 7, r - 96))
                behind = jnp.where(r == 0, 8, jnp.where(r == 255, 9, 176 - r))
                first = jnp.where(front, ahead, behind)
                for t in range(CT):
                    window[pl.ds(t * PIECE, PIECE), :] = near[k][(first + t) & 63]

        @pl.when(front)
        def _():
            for v in range(NV):
                ghost_hi[k, v] = window[pl.ds(v, CT, stride=PIECE), :]

        @pl.when(aft)
        def _():
            for v in range(NV):
                ghost_lo[k, v] = window[pl.ds(v, CT, stride=PIECE), :]

        down, up = axial_copies(k)

        @pl.when(has_hi)
        def _():
            down.wait_recv()

        @pl.when(has_lo)
        def _():
            up.wait_recv()

    lane = lax.broadcasted_iota(jnp.int32, (CZ, NR), 1)
    line = lax.broadcasted_iota(jnp.int32, (CZ, NR), 0)

    def plane(k, t):
        state = states[k]
        base = pl.multiple_of(t * CZ, CZ)
        here = pl.ds(pl.multiple_of(base + CZ, CZ), CZ)
        center = [state[v, here, :] for v in range(NV)]
        advection = [None] * NV
        total = [None] * NV
        for d in range(3):
            for j in range(NV):
                c = center[j]
                if d == 0:
                    upper = state[j, pl.ds(pl.multiple_of(base + 2 * CZ, CZ), CZ), :]
                    lower = state[j, pl.ds(base, CZ), :]
                elif d == 1:
                    upper = jnp.where(line == CZ - 1, 0.0, pltpu.roll(c, CZ - 1, 0))
                    lower = jnp.where(line == 0, 0.0, pltpu.roll(c, 1, 0))
                else:
                    upper = jnp.where(lane == NR - 1, 0.0, pltpu.roll(c, NR - 1, 1))
                    lower = jnp.where(lane == 0, 0.0, pltpu.roll(c, 1, 1))
                both = upper + lower
                total[j] = both if d == 0 else total[j] + both
                slope = upper - lower
                for i in range(NV):
                    term = (0.5 * jac_ref[i, d, j]) * slope
                    advection[i] = term if advection[i] is None else advection[i] + term
        drag = damp_ref[pl.ds(base, CZ), :] + 6.0 * viscosity
        for i in range(NV):
            rate = viscosity * total[i] - advection[i] - drag * center[i]
            start = s1[i, here, :] if k else center[i]
            if k < 3:
                scale = time_step if k == 2 else 0.5 * time_step
                states[k + 1][i, here, :] = start + scale * rate
            else:
                mix = (s2[i, here, :] + 2.0 * s3[i, here, :] + center[i] - start) * (1.0 / 3.0)
                new_ref[i, pl.ds(base, CZ), :] = mix + (time_step / 6.0) * rate

    def correct(k):
        for side, ghost in ((0, ghost_lo), (1, ghost_hi)):
            sign = 0.5 if side == 0 else -0.5
            row = 0 if side == 0 else CZ - 1
            values = [ghost[k, j] for j in range(NV)]
            for i in range(NV):
                rate = viscosity * values[i]
                for j in range(NV):
                    rate = rate + (sign * jac_ref[i, 1, j]) * values[j]
                if k < 3:
                    scale = time_step if k == 2 else 0.5 * time_step
                    where = pl.ds(CZ + row, CT, stride=CZ)
                    states[k + 1][i, where, :] = states[k + 1][i, where, :] + scale * rate
                else:
                    where = pl.ds(row, CT, stride=CZ)
                    new_ref[i, where, :] = new_ref[i, where, :] + (time_step / 6.0) * rate

    pick = (lax.broadcasted_iota(jnp.int32, (8, NR), 1) == NR // 2).astype(jnp.float32)

    def sample(k):
        state = states[k]
        total = None
        for v in range(NV):
            column = lax.dot_general(
                pick,
                state[v, pl.ds(CZ, ROWS), :],
                (((1,), (1,)), ((), ())),
                precision=lax.Precision.HIGHEST,
                preferred_element_type=jnp.float32,
            )
            term = column[0:1] * weight[v : v + 1, :]
            total = term if total is None else total + term
        for block in range(4):
            part = total[:, block * 128 : (block + 1) * 128]
            if k == 3:
                parcel2[block : block + 1, :] = part
            elif k == 2:
                parcel1[block : block + 1, :] = part
            else:
                parcel0[2 * block + k : 2 * block + k + 1, :] = part

    def spread(row):
        return jnp.broadcast_to(row, (8, 128))

    fine = lax.broadcasted_iota(jnp.int32, (32, 128), 0).astype(jnp.float32).astype(jnp.bfloat16)
    place = lax.broadcasted_iota(jnp.int32, (8, 128), 0)
    which_sample = place % 4

    def prepare(n):
        @pl.loop(0, NA)
        def _(m):
            fine_bin = (bin_ref[m, n] & 31).astype(jnp.float32)
            for o in range(2):
                columns = []
                for c in range(4):
                    row = 2 * c + o
                    within = jnp.broadcast_to(fine_bin[row : row + 1], (32, 128)).astype(jnp.bfloat16)
                    columns.append(jnp.where(within == fine, jnp.bfloat16(1), jnp.bfloat16(0)))
                selector_ref[n, m, o] = jnp.concatenate(columns, 1)

    def widen():
        spot = lax.broadcasted_iota(jnp.int32, (128, 5 * 128), 0)
        part_of = lax.broadcasted_iota(jnp.int32, (128, 5 * 128), 1) // 128
        table = (spot == part_of).astype(jnp.bfloat16)
        for n in range(NB):
            wide_ref[n] = jnp.dot(
                lists_ref[n].astype(jnp.bfloat16), table, preferred_element_type=jnp.float32
            )

    def chosen(n, m, c, blocks):
        listed = spread(wide_ref[n, m : m + 1, c * 128 : (c + 1) * 128])
        count = spread(wide_ref[n, m : m + 1, 4 * 128 : 5 * 128])
        picked = jnp.zeros((8, 128), jnp.float32)
        for block in range(4):
            picked = jnp.where(listed == block, blocks[block], picked)
        return jnp.where(count > c, picked, 0.0)

    def halves(part):
        head = part.astype(jnp.bfloat16).astype(jnp.float32)
        return jnp.concatenate([head, part - head], 0).astype(jnp.bfloat16)

    def against(weights, n, m, o):
        return lax.dot_general(
            jnp.concatenate(weights, 1),
            selector_ref[n, m, o],
            (((1,), (1,)), ((), ())),
            preferred_element_type=jnp.float32,
        )

    def bin_first(n):
        low = place < 4
        sign = jnp.where(low, -1.0, 1.0).astype(jnp.float32)
        shift = jnp.where(low, 1.0, 0.0).astype(jnp.float32)
        zero = jnp.zeros((16, 128), jnp.bfloat16)
        sums = [jnp.zeros((64, 32), jnp.float32)] * 2
        for m in range(NA):
            gain = gain_ref[m, n]
            fraction = fraction_ref[m, n]
            coarse_bin = (bin_ref[m, n] >> 5).astype(jnp.float32)
            early = early_ref[n, m % 2, m // 2]
            middle = middle_ref[n, m % 2, m // 2]
            blocks = []
            for block in range(4):
                later = jnp.where(which_sample == 2, spread(middle[block : block + 1]), 0.0)
                later = jnp.where(which_sample == 1, spread(early[2 * block + 1 : 2 * block + 2]), later)
                blocks.append(jnp.where(which_sample == 0, spread(early[2 * block : 2 * block + 1]), later))
            weights = [[], []]
            for c in range(4):
                received = chosen(n, m, c, blocks)
                for o in range(2):
                    row = slice(2 * c + o, 2 * c + o + 1)
                    both = halves(received * (spread(gain[row]) * (spread(fraction[row]) * sign + shift)))
                    coarse = jnp.broadcast_to(coarse_bin[row], (16, 128)).astype(jnp.bfloat16)
                    weights[o].append(
                        jnp.concatenate([jnp.where(coarse == jnp.bfloat16(q), both, zero) for q in range(4)], 0)
                    )
            for o in range(2):
                sums[o] = sums[o] + against(weights[o], n, m, o)
        for o in range(2):
            total[o] += sums[o]

    def bin_last(n):
        part = place % 2
        group = (place // 2).astype(jnp.float32)
        sign = jnp.where(part == 0, -1.0, 1.0).astype(jnp.float32)
        shift = jnp.where(part == 0, 1.0, 0.0).astype(jnp.float32)
        sums = [jnp.zeros((16, 32), jnp.float32)] * 2
        for m in range(NA):
            gain = gain_ref[m, n]
            fraction = fraction_ref[m, n]
            coarse_bin = (bin_ref[m, n] >> 5).astype(jnp.float32)
            late = late_ref[n, m % 2, m // 2]
            blocks = [spread(late[block : block + 1]) for block in range(4)]
            weights = [[], []]
            for c in range(4):
                received = chosen(n, m, c, blocks)
                for o in range(2):
                    row = slice(2 * c + o, 2 * c + o + 1)
                    scale = spread(gain[row]) * (spread(fraction[row]) * sign + shift)
                    scale = jnp.where(spread(coarse_bin[row]) == group, scale, 0.0)
                    weights[o].append(halves(received * scale))
            for o in range(2):
                sums[o] = sums[o] + against(weights[o], n, m, o)
        for o in range(2):
            last_total[o] += sums[o]

    def emit():
        for o in range(2):
            signal = jnp.zeros((1, NBIN), jnp.float32)
            for q in range(8):
                if q % 4 < 3:
                    rows = [(16 * g + q, 16 * g + 8 + q) for g in range(4)]
                    source = total
                else:
                    rows = [(2 * g + q // 4, 8 + 2 * g + q // 4) for g in range(4)]
                    source = last_total
                whole = jnp.concatenate([source[o, h : h + 1, :] + source[o, l : l + 1, :] for h, l in rows], 1)
                offset = q % 4 + q // 4
                signal = signal + (pltpu.roll(whole, offset, 1) if offset else whole)
            signal_ref[o : o + 1, :] = signal

    total[...] = jnp.zeros_like(total)
    last_total[...] = jnp.zeros_like(last_total)
    for load in loads[:7]:
        load.wait()
    for t in range(CT):
        weight[0:NV, t * CZ : (t + 1) * CZ] = fw_ref[:, t, :]
    rows = jnp.concatenate([list_ref[...], count_ref[...], jnp.zeros((3, NR), jnp.int32)], 0).astype(jnp.float32)
    places = lax.broadcasted_iota(jnp.int32, (8, NR), 0) == lax.broadcasted_iota(jnp.int32, (8, NR), 1)
    list_out[...] = lax.dot_general(
        rows,
        places.astype(jnp.float32),
        (((0,), (0,)), ((), ())),
        precision=lax.Precision.HIGHEST,
        preferred_element_type=jnp.float32,
    )
    sample(0)
    pl.semaphore_wait(barrier, jnp.where(interface, NA - 1 + NB - 1 + NA, NA - 1 + NB - 1))
    send_edges(0)
    list_first()
    def between(k):
        if k == 0:
            for load in loads[7:]:
                load.wait()

        @pl.loop(2 * k, 2 * k + 2)
        def _(n):
            prepare(n)

        if k == 2:
            list_wait()
            widen()
        if k == 3:
            line_start(2)
            pair_start(1)
        down, up = theta_copies(k)
        down.wait_recv()
        up.wait_recv()

    for k in range(4):
        @pl.loop(0, CT)
        def _(step):
            if k == free:
                @pl.when(step == CT // 2)
                def _():
                    relay()

            @pl.when(step == CT - 2)
            def _():
                between(k)

            plane(k, lax.rem(step + 1, CT))

        land(k)
        correct(k)
        if k < 3:
            send_edges(k + 1)
        if k == 0:
            sample(1)
            ring_start(0)
            list_second()
        elif k == 1:
            sample(2)
            ring_start(1)
            line_start(0)
        elif k == 2:
            sample(3)
            ring_start(2)
            line_start(1)
            pair_start(0)

    for which in range(2):
        pair_copy(which).wait_recv()

    @pl.loop(0, NB)
    def _(n):
        @pl.when(n == NB // 2)
        def _():
            pair_start(2)

        bin_first(n)

    pair_copy(2).wait_recv()

    @pl.loop(0, NB)
    def _(n):
        bin_last(n)

    emit()
    for which in range(3):
        wait_rows(gathers[which].at[0, 0, pl.ds(0, NA // 2 - 1)], ring_send.at[which])
        wait_rows(gathers[which].at[pl.ds(0, NB - 1), 0], line_send.at[which])
        pair_copy(which).wait_send()
    for k in range(4):
        down, up = theta_copies(k)
        down.wait_send()
        up.wait_send()
        down, up = axial_copies(k)

        @pl.when(has_lo)
        def _():
            down.wait_send()

        @pl.when(has_hi)
        def _():
            up.wait_send()

        @pl.when(interface)
        def _():
            if k == free:
                wait_rows(row_out.at[k], row_send.at[k])
                wait_rows(row_sel.at[pl.ds(0, NA - 1)], sel_send.at[0])
            else:
                wait_rows(near[k].at[pl.ds(0, 56), pl.ds(0, NV), :], row_send.at[k])


def step_call(
    free, x, damping, jacobians, face_weight, phase_shift, lists, counts, bins, fractions, gains
):
    vmem = pl.BlockSpec(memory_space=pltpu.VMEM)
    hbm = pl.BlockSpec(memory_space=pltpu.HBM)
    state = pltpu.VMEM((NV, PAD, NR), jnp.float32)
    edge = pltpu.VMEM((4, NV, CT, NR), jnp.float32)
    row = pltpu.VMEM((NA, PIECE, NR), jnp.float32)
    dma = pltpu.SemaphoreType.DMA
    return pl.pallas_call(
        functools.partial(step_kernel, free),
        out_shape=(
            jax.ShapeDtypeStruct((NV, ROWS, NR), jnp.float32),
            jax.ShapeDtypeStruct((2, NBIN), jnp.float32),
        ),
        in_specs=[hbm] * 10,
        out_specs=(vmem,) * 2,
        scratch_shapes=[
            pltpu.VMEM((NB, NA, NR), jnp.float32),
            pltpu.VMEM((NB, 2, NA // 2, 8, NR), jnp.float32),
            pltpu.VMEM((NB, 2, NA // 2, 4, NR), jnp.float32),
            pltpu.VMEM((NB, 2, NA // 2, 4, NR), jnp.float32),
            pltpu.VMEM((NA, NB, PIECE, 128), jnp.int32),
            pltpu.VMEM((NA, NB, PIECE, 128), jnp.float32),
            pltpu.VMEM((NA, NB, PIECE, 128), jnp.float32),
            pltpu.VMEM((NB, NA, 2, 32, 512), jnp.bfloat16),
            pltpu.VMEM((NB, NA, 5 * 128), jnp.float32),
            pltpu.VMEM((2, 64, 32), jnp.float32),
            pltpu.VMEM((2, 16, 32), jnp.float32),
            pltpu.VMEM((ROWS, NR), jnp.float32),
            pltpu.SMEM((NV, 3, NV), jnp.float32),
            pltpu.VMEM((NV, CT, CZ), jnp.float32),
            pltpu.SMEM((4,), jnp.int32),
            pltpu.VMEM((4, NR), jnp.int32),
            pltpu.VMEM((1, NR), jnp.int32),
            pltpu.VMEM((8, ROWS), jnp.float32),
        ]
        + [state] * 4
        + [edge] * 4
        + [pltpu.VMEM((4, CT, PIECE, NR), jnp.float32), row, row, row]
        + [pltpu.VMEM((64, PIECE, NR), jnp.float32)] * 3
        + [pltpu.VMEM((CT * PIECE, NR), jnp.float32)]
        + [pltpu.VMEM((NA * NB, NR), jnp.float32)] * 2
        + [pltpu.VMEM((NB, NA, NR), jnp.float32)]
        + [pltpu.VMEM((rows, NR), jnp.float32) for rows in (8, 4, 4)]
        + [dma((10,)), dma((4, 2)), dma((4, 2)), dma((4, 2)), dma((4, 2))]
        + [dma((4,)), dma((4,)), dma((1,)), dma((1,))]
        + [dma((2,))] * 2
        + [dma((3,))] * 6,
        compiler_params=pltpu.CompilerParams(
            collective_id=free, has_side_effects=True, vmem_limit_bytes=44 << 20
        ),
        name="substeps%d" % free,
    )(x, damping, jacobians, face_weight, phase_shift, lists, counts, bins, fractions, gains)


def local(
    flow_state,
    damping,
    jacobians,
    face_weight,
    phase_shift,
    face_list,
    face_count,
    arrival_bin,
    arrival_fraction,
    arrival_gain,
):
    zero = phase_shift == 0
    last = phase_shift == CT * NA - 1
    opposite = jnp.logical_and(phase_shift >= 128, phase_shift < 144)
    apart = jnp.logical_not(jnp.eye(4, dtype=bool))

    def elsewhere(flags):
        return jnp.any(jnp.logical_and(apart, flags[None, :]), axis=1)

    rest = elsewhere(zero) & elsewhere(last) & elsewhere(opposite)
    free = jnp.min(jnp.where(rest, jnp.arange(4, dtype=jnp.int32), 3))
    new_state, signal = lax.switch(
        free,
        [functools.partial(step_call, k) for k in range(4)],
        flow_state.reshape(NV, ROWS, NR),
        damping.reshape(ROWS, NR),
        jnp.transpose(jacobians, (1, 0, 2)),
        face_weight,
        phase_shift,
        face_list[0].T,
        face_count,
        arrival_bin.reshape(NA, NB, PIECE, 128),
        arrival_fraction.reshape(NA, NB, PIECE, 128),
        arrival_gain.reshape(NA, NB, PIECE, 128),
    )
    return new_state.reshape(NV, CT, CZ, NR), signal


def solution(mesh):
    return jax.shard_map(
        local,
        mesh=mesh,
        in_specs=(
            P(None, "sector", "axial", None),
            P("sector", "axial", None),
            P(),
            P(None, "sector", "axial"),
            P(),
            P(("sector", "axial"), None, None),
            P(("sector", "axial"), None),
            P(("sector", "axial"), None, None, None, None),
            P(("sector", "axial"), None, None, None, None),
            P(("sector", "axial"), None, None, None, None),
        ),
        out_specs=(P(None, "sector", "axial", None), P(("sector", "axial"), None)),
        check_vma=False,
    )
```

```python
import functools

import jax
import jax.numpy as jnp
from jax import lax
from jax.experimental import pallas as pl
from jax.experimental.pallas import tpu as pltpu
from jax.sharding import PartitionSpec as P

NV = 5
NA = 16
NB = 8
CT = 16
CZ = 32
NR = 128
ROWS = CT * CZ
PAD = ROWS + 2 * CZ
NBIN = 128
PIECE = 8

time_step = 0.3
viscosity = 0.05

MESH = pl.DeviceIdType.MESH


def wait_rows(ref, sem):
    pltpu.make_async_copy(ref, ref, sem).wait()


def step_kernel(
    free,
    x_hbm,
    damp_hbm,
    jac_hbm,
    fw_hbm,
    shift_hbm,
    list_hbm,
    count_hbm,
    bin_hbm,
    fraction_hbm,
    gain_hbm,
    new_ref,
    signal_ref,
    lists_ref,
    early_ref,
    middle_ref,
    late_ref,
    bin_ref,
    fraction_ref,
    gain_ref,
    selector_ref,
    first_scale,
    last_scale,
    wide_ref,
    total,
    last_total,
    damp_ref,
    jac_ref,
    fw_ref,
    shift_ref,
    list_ref,
    count_ref,
    weight,
    s1,
    s2,
    s3,
    s4,
    edge_lo,
    edge_hi,
    ghost_lo,
    ghost_hi,
    row_out,
    row_sel,
    held,
    incoming,
    near1,
    near2,
    near3,
    window,
    list_out,
    list_mid,
    list_stage,
    parcel0,
    parcel1,
    parcel2,
    load_sem,
    theta_send,
    theta_recv,
    axial_send,
    axial_recv,
    row_send,
    row_recv,
    sel_send,
    sel_recv,
    list_send,
    list_recv,
    ring_send,
    ring_recv,
    line_send,
    line_recv,
    pair_send,
    pair_recv,
):
    a = lax.axis_index("sector")
    b = lax.axis_index("axial")
    front = b == NB // 2 - 1
    aft = b == NB // 2
    interface = jnp.logical_or(front, aft)
    other = jnp.where(front, NB // 2, NB // 2 - 1)
    has_lo = jnp.logical_and(b > 0, jnp.logical_not(aft))
    has_hi = jnp.logical_and(b < NB - 1, jnp.logical_not(front))
    states = [s1, s2, s3, s4]
    direct = [k for k in range(4) if k != free]
    near = dict(zip(direct, (near1, near2, near3)))
    parcels = [parcel0, parcel1, parcel2]
    gathers = [early_ref, middle_ref, late_ref]

    loads = [
        pltpu.make_async_copy(source, target, load_sem.at[n])
        for n, (source, target) in enumerate(
            (
                (x_hbm, s1.at[:, pl.ds(CZ, ROWS), :]),
                (fw_hbm, fw_ref),
                (list_hbm, list_ref),
                (count_hbm, count_ref),
                (shift_hbm, shift_ref),
                (jac_hbm, jac_ref),
                (damp_hbm, damp_ref),
                (bin_hbm, bin_ref),
                (fraction_hbm, fraction_ref),
                (gain_hbm, gain_ref),
            )
        )
    ]
    for load in loads:
        load.start()

    barrier = pltpu.get_barrier_semaphore()

    @pl.loop(1, NA)
    def _(step):
        pl.semaphore_signal(barrier, inc=1, device_id=(lax.rem(a + step, NA), b), device_id_type=MESH)

    @pl.loop(1, NB)
    def _(step):
        pl.semaphore_signal(barrier, inc=1, device_id=(a, lax.rem(b + step, NB)), device_id_type=MESH)

    @pl.when(interface)
    def _():
        @pl.loop(0, NA)
        def _(step):
            pl.semaphore_signal(barrier, inc=1, device_id=(step, other), device_id_type=MESH)

    window[...] = jnp.zeros_like(window)
    weight[...] = jnp.zeros_like(weight)
    for k in range(4):
        @pl.when(b == 0)
        def _():
            ghost_lo[k] = jnp.zeros((NV, CT, NR), jnp.float32)

        @pl.when(b == NB - 1)
        def _():
            ghost_hi[k] = jnp.zeros((NV, CT, NR), jnp.float32)


    def list_rows(n):
        return pl.ds(pl.multiple_of(n * NB, NB), NB)

    def list_first():
        list_mid[list_rows(a), :] = list_out[list_rows(a), :]

        @pl.loop(1, NA)
        def _(step):
            to = lax.rem(a + step, NA)
            pltpu.make_async_remote_copy(
                src_ref=list_out.at[list_rows(to), :],
                dst_ref=list_mid.at[list_rows(a), :],
                send_sem=list_send.at[0],
                recv_sem=list_recv.at[0],
                device_id=(to, b),
                device_id_type=MESH,
            ).start()

    def list_second():
        wait_rows(list_mid.at[pl.ds(0, (NA - 1) * NB), :], list_recv.at[0])
        for n in range(NB):
            list_stage[n] = list_mid[pl.ds(n, NA, stride=NB), :]
        lists_ref[b] = list_stage[b]

        @pl.loop(1, NB)
        def _(step):
            to = lax.rem(b + step, NB)
            pltpu.make_async_remote_copy(
                src_ref=list_stage.at[to],
                dst_ref=lists_ref.at[b],
                send_sem=list_send.at[1],
                recv_sem=list_recv.at[1],
                device_id=(a, to),
                device_id_type=MESH,
            ).start()

    def list_wait():
        wait_rows(lists_ref.at[pl.ds(0, NB - 1)], list_recv.at[1])
        wait_rows(list_mid.at[pl.ds(0, (NA - 1) * NB), :], list_send.at[0])
        wait_rows(lists_ref.at[pl.ds(0, NB - 1)], list_send.at[1])

    core = lax.rem(a, 2)
    chip = a // 2

    def ring_start(which):
        gathers[which][b, core, chip] = parcels[which][...]

        @pl.loop(1, NA // 2)
        def _(step):
            pltpu.make_async_remote_copy(
                src_ref=parcels[which],
                dst_ref=gathers[which].at[b, core, chip],
                send_sem=ring_send.at[which],
                recv_sem=ring_recv.at[which],
                device_id=(lax.rem(a + 2 * step, NA), b),
                device_id_type=MESH,
            ).start()

    def line_start(which):
        wait_rows(gathers[which].at[0, 0, pl.ds(0, NA // 2 - 1)], ring_recv.at[which])

        @pl.loop(1, NB)
        def _(step):
            pltpu.make_async_remote_copy(
                src_ref=gathers[which].at[b, core],
                dst_ref=gathers[which].at[b, core],
                send_sem=line_send.at[which],
                recv_sem=line_recv.at[which],
                device_id=(a, lax.rem(b + step, NB)),
                device_id_type=MESH,
            ).start()

    def pair_copy(which):
        return pltpu.make_async_remote_copy(
            src_ref=gathers[which].at[:, core],
            dst_ref=gathers[which].at[:, core],
            send_sem=pair_send.at[which],
            recv_sem=pair_recv.at[which],
            device_id=(a + 1 - 2 * core, b),
            device_id_type=MESH,
        )

    def pair_start(which):
        wait_rows(gathers[which].at[pl.ds(0, NB - 1), 0], line_recv.at[which])
        pair_copy(which).start()

    def theta_copies(k):
        state = states[k]
        down = pltpu.make_async_remote_copy(
            src_ref=state.at[:, pl.ds(CZ, CZ), :],
            dst_ref=state.at[:, pl.ds(CZ + ROWS, CZ), :],
            send_sem=theta_send.at[k, 0],
            recv_sem=theta_recv.at[k, 0],
            device_id=(lax.rem(a + NA - 1, NA), b),
            device_id_type=MESH,
        )
        up = pltpu.make_async_remote_copy(
            src_ref=state.at[:, pl.ds(ROWS, CZ), :],
            dst_ref=state.at[:, pl.ds(0, CZ), :],
            send_sem=theta_send.at[k, 1],
            recv_sem=theta_recv.at[k, 1],
            device_id=(lax.rem(a + 1, NA), b),
            device_id_type=MESH,
        )
        return down, up

    def axial_copies(k):
        down = pltpu.make_async_remote_copy(
            src_ref=edge_lo.at[k],
            dst_ref=ghost_hi.at[k],
            send_sem=axial_send.at[k, 0],
            recv_sem=axial_recv.at[k, 0],
            device_id=(a, jnp.maximum(b - 1, 0)),
            device_id_type=MESH,
        )
        up = pltpu.make_async_remote_copy(
            src_ref=edge_hi.at[k],
            dst_ref=ghost_lo.at[k],
            send_sem=axial_send.at[k, 1],
            recv_sem=axial_recv.at[k, 1],
            device_id=(a, jnp.minimum(b + 1, NB - 1)),
            device_id_type=MESH,
        )
        return down, up

    def send_edges(k):
        state = states[k]

        @pl.when(front)
        def _():
            for v in range(NV):
                window[pl.ds(v, CT, stride=PIECE), :] = state[v, pl.ds(CZ + CZ - 1, CT, stride=CZ), :]

        @pl.when(aft)
        def _():
            for v in range(NV):
                window[pl.ds(v, CT, stride=PIECE), :] = state[v, pl.ds(CZ, CT, stride=CZ), :]

        @pl.when(interface)
        def _():
            for t in range(CT):
                row_out[k, t] = window[pl.ds(t * PIECE, PIECE), :]

            if k == free:
                @pl.loop(0, CT)
                def _(t):
                    pltpu.make_async_remote_copy(
                        src_ref=row_out.at[k, t],
                        dst_ref=held.at[a],
                        send_sem=row_send.at[k],
                        recv_sem=row_recv.at[k],
                        device_id=(t, other),
                        device_id_type=MESH,
                    ).start()
            else:
                for target, first, place, count in (
                    (a, 0, 8, 16),
                    (a + 8, 0, jnp.where(front, 48, 32), 16),
                    (a + jnp.where(front, 9, 7), 0, jnp.where(front, 32, 48), 16),
                    (a + jnp.where(front, NA - 1, 1), jnp.where(front, 0, 8), jnp.where(front, 24, 0), 8),
                ):
                    pltpu.make_async_remote_copy(
                        src_ref=row_out.at[k, pl.ds(first, count), pl.ds(0, NV), :],
                        dst_ref=near[k].at[pl.ds(place, count), pl.ds(0, NV), :],
                        send_sem=row_send.at[k],
                        recv_sem=row_recv.at[k],
                        device_id=(lax.rem(target, NA), other),
                        device_id_type=MESH,
                    ).start()

        down, up = theta_copies(k)
        down.start()
        up.start()
        down, up = axial_copies(k)

        @pl.when(has_lo)
        def _():
            for v in range(NV):
                edge_lo[k, v] = state[v, pl.ds(CZ, CT, stride=CZ), :]
            down.start()

        @pl.when(has_hi)
        def _():
            for v in range(NV):
                edge_hi[k, v] = state[v, pl.ds(CZ + CZ - 1, CT, stride=CZ), :]
            up.start()

    def turn(k):
        r = shift_ref[k]
        return jnp.where(front, r, (CT * NA - r) & (CT * NA - 1))

    def relay():
        @pl.when(interface)
        def _():
            wait_rows(held, row_recv.at[free])
            first = (turn(free) - a + CT - 1) >> 4

            @pl.loop(0, NA)
            def _(d):
                row_sel[d] = held[(d + first) & (NA - 1)]

            @pl.loop(1, NA)
            def _(step):
                d = lax.rem(a + step, NA)
                pltpu.make_async_remote_copy(
                    src_ref=row_sel.at[d],
                    dst_ref=incoming.at[a],
                    send_sem=sel_send.at[0],
                    recv_sem=sel_recv.at[0],
                    device_id=(d, b),
                    device_id_type=MESH,
                ).start()
            incoming[a] = row_sel[a]

    def land(k):
        @pl.when(interface)
        def _():
            if k == free:
                wait_rows(incoming.at[pl.ds(0, NA - 1)], sel_recv.at[0])
                r = turn(k)
                for t in range(CT):
                    window[pl.ds(t * PIECE, PIECE), :] = incoming[(r + t) & (CT - 1)]
            else:
                wait_rows(near[k].at[pl.ds(0, 56), pl.ds(0, NV), :], row_recv.at[k])
                r = shift_ref[k]
                ahead = jnp.where(r == 0, 8, jnp.where(r == 255, 7, r - 96))
                behind = jnp.where(r == 0, 8, jnp.where(r == 255, 9, 176 - r))
                first = jnp.where(front, ahead, behind)
                for t in range(CT):
                    window[pl.ds(t * PIECE, PIECE), :] = near[k][(first + t) & 63]

        @pl.when(front)
        def _():
            for v in range(NV):
                ghost_hi[k, v] = window[pl.ds(v, CT, stride=PIECE), :]

        @pl.when(aft)
        def _():
            for v in range(NV):
                ghost_lo[k, v] = window[pl.ds(v, CT, stride=PIECE), :]

        down, up = axial_copies(k)

        @pl.when(has_hi)
        def _():
            down.wait_recv()

        @pl.when(has_lo)
        def _():
            up.wait_recv()

    lane = lax.broadcasted_iota(jnp.int32, (CZ, NR), 1)
    line = lax.broadcasted_iota(jnp.int32, (CZ, NR), 0)

    def plane(k, t):
        state = states[k]
        base = pl.multiple_of(t * CZ, CZ)
        here = pl.ds(pl.multiple_of(base + CZ, CZ), CZ)
        center = [state[v, here, :] for v in range(NV)]
        advection = [None] * NV
        total = [None] * NV
        for d in range(3):
            for j in range(NV):
                c = center[j]
                if d == 0:
                    upper = state[j, pl.ds(pl.multiple_of(base + 2 * CZ, CZ), CZ), :]
                    lower = state[j, pl.ds(base, CZ), :]
                elif d == 1:
                    upper = jnp.where(line == CZ - 1, 0.0, pltpu.roll(c, CZ - 1, 0))
                    lower = jnp.where(line == 0, 0.0, pltpu.roll(c, 1, 0))
                else:
                    upper = jnp.where(lane == NR - 1, 0.0, pltpu.roll(c, NR - 1, 1))
                    lower = jnp.where(lane == 0, 0.0, pltpu.roll(c, 1, 1))
                both = upper + lower
                total[j] = both if d == 0 else total[j] + both
                slope = upper - lower
                for i in range(NV):
                    term = (0.5 * jac_ref[i, d, j]) * slope
                    advection[i] = term if advection[i] is None else advection[i] + term
        drag = damp_ref[pl.ds(base, CZ), :] + 6.0 * viscosity
        for i in range(NV):
            rate = viscosity * total[i] - advection[i] - drag * center[i]
            start = s1[i, here, :] if k else center[i]
            if k < 3:
                scale = time_step if k == 2 else 0.5 * time_step
                states[k + 1][i, here, :] = start + scale * rate
            else:
                mix = (s2[i, here, :] + 2.0 * s3[i, here, :] + center[i] - start) * (1.0 / 3.0)
                new_ref[i, pl.ds(base, CZ), :] = mix + (time_step / 6.0) * rate

    def correct(k):
        for side, ghost in ((0, ghost_lo), (1, ghost_hi)):
            sign = 0.5 if side == 0 else -0.5
            row = 0 if side == 0 else CZ - 1
            values = [ghost[k, j] for j in range(NV)]
            for i in range(NV):
                rate = viscosity * values[i]
                for j in range(NV):
                    rate = rate + (sign * jac_ref[i, 1, j]) * values[j]
                if k < 3:
                    scale = time_step if k == 2 else 0.5 * time_step
                    where = pl.ds(CZ + row, CT, stride=CZ)
                    states[k + 1][i, where, :] = states[k + 1][i, where, :] + scale * rate
                else:
                    where = pl.ds(row, CT, stride=CZ)
                    new_ref[i, where, :] = new_ref[i, where, :] + (time_step / 6.0) * rate

    pick = (lax.broadcasted_iota(jnp.int32, (8, NR), 1) == NR // 2).astype(jnp.float32)

    def sample(k):
        state = states[k]
        total = None
        for v in range(NV):
            column = lax.dot_general(
                pick,
                state[v, pl.ds(CZ, ROWS), :],
                (((1,), (1,)), ((), ())),
                precision=lax.Precision.HIGHEST,
                preferred_element_type=jnp.float32,
            )
            term = column[0:1] * weight[v : v + 1, :]
            total = term if total is None else total + term
        for block in range(4):
            part = total[:, block * 128 : (block + 1) * 128]
            if k == 3:
                parcel2[block : block + 1, :] = part
            elif k == 2:
                parcel1[block : block + 1, :] = part
            else:
                parcel0[2 * block + k : 2 * block + k + 1, :] = part

    def spread(row):
        return jnp.broadcast_to(row, (8, 128))

    fine = lax.broadcasted_iota(jnp.int32, (32, 128), 0).astype(jnp.float32).astype(jnp.bfloat16)
    place = lax.broadcasted_iota(jnp.int32, (8, 128), 0)
    which_sample = place % 4

    first_sign = jnp.where(place < 4, -1.0, 1.0).astype(jnp.float32)
    first_shift = jnp.where(place < 4, 1.0, 0.0).astype(jnp.float32)
    last_sign = jnp.where(place % 2 == 0, -1.0, 1.0).astype(jnp.float32)
    last_shift = jnp.where(place % 2 == 0, 1.0, 0.0).astype(jnp.float32)
    group = (place // 2).astype(jnp.float32)

    def prepare(n):
        @pl.loop(0, NA)
        def _(m):
            fine_bin = (bin_ref[m, n] & 31).astype(jnp.float32)
            for o in range(2):
                columns = []
                for c in range(4):
                    row = 2 * c + o
                    within = jnp.broadcast_to(fine_bin[row : row + 1], (32, 128)).astype(jnp.bfloat16)
                    columns.append(jnp.where(within == fine, jnp.bfloat16(1), jnp.bfloat16(0)))
                selector_ref[n, m, o] = jnp.concatenate(columns, 1)
            coarse_bin = (bin_ref[m, n] >> 5).astype(jnp.float32)
            gains = gain_ref[m, n]
            fractions = fraction_ref[m, n]
            for row in range(PIECE):
                gain = spread(gains[row : row + 1])
                fraction = spread(fractions[row : row + 1])
                first_scale[n, m, row] = gain * (fraction * first_sign + first_shift)
                scale = gain * (fraction * last_sign + last_shift)
                last_scale[n, m, row] = jnp.where(spread(coarse_bin[row : row + 1]) == group, scale, 0.0)

    def widen():
        spot = lax.broadcasted_iota(jnp.int32, (128, 5 * 128), 0)
        part_of = lax.broadcasted_iota(jnp.int32, (128, 5 * 128), 1) // 128
        table = (spot == part_of).astype(jnp.bfloat16)
        for n in range(NB):
            wide_ref[n] = jnp.dot(
                lists_ref[n].astype(jnp.bfloat16), table, preferred_element_type=jnp.float32
            )

    def chosen(n, m, c, blocks):
        listed = spread(wide_ref[n, m : m + 1, c * 128 : (c + 1) * 128])
        count = spread(wide_ref[n, m : m + 1, 4 * 128 : 5 * 128])
        picked = jnp.zeros((8, 128), jnp.float32)
        for block in range(4):
            picked = jnp.where(listed == block, blocks[block], picked)
        return jnp.where(count > c, picked, 0.0)

    def halves(part):
        head = part.astype(jnp.bfloat16).astype(jnp.float32)
        return jnp.concatenate([head, part - head], 0).astype(jnp.bfloat16)

    def against(weights, n, m, o):
        return lax.dot_general(
            jnp.concatenate(weights, 1),
            selector_ref[n, m, o],
            (((1,), (1,)), ((), ())),
            preferred_element_type=jnp.float32,
        )

    def bin_first(n):
        zero = jnp.zeros((16, 128), jnp.bfloat16)
        sums = [jnp.zeros((64, 32), jnp.float32)] * 2
        for m in range(NA):
            coarse_bin = (bin_ref[m, n] >> 5).astype(jnp.float32)
            early = early_ref[n, m % 2, m // 2]
            middle = middle_ref[n, m % 2, m // 2]
            blocks = []
            for block in range(4):
                later = jnp.where(which_sample == 2, spread(middle[block : block + 1]), 0.0)
                later = jnp.where(which_sample == 1, spread(early[2 * block + 1 : 2 * block + 2]), later)
                blocks.append(jnp.where(which_sample == 0, spread(early[2 * block : 2 * block + 1]), later))
            weights = [[], []]
            for c in range(4):
                received = chosen(n, m, c, blocks)
                for o in range(2):
                    row = slice(2 * c + o, 2 * c + o + 1)
                    both = halves(received * first_scale[n, m, 2 * c + o])
                    coarse = jnp.broadcast_to(coarse_bin[row], (16, 128)).astype(jnp.bfloat16)
                    weights[o].append(
                        jnp.concatenate([jnp.where(coarse == jnp.bfloat16(q), both, zero) for q in range(4)], 0)
                    )
            for o in range(2):
                sums[o] = sums[o] + against(weights[o], n, m, o)
        for o in range(2):
            total[o] += sums[o]

    def bin_last(n):
        sums = [jnp.zeros((16, 32), jnp.float32)] * 2
        for m in range(NA):
            late = late_ref[n, m % 2, m // 2]
            blocks = [spread(late[block : block + 1]) for block in range(4)]
            weights = [[], []]
            for c in range(4):
                received = chosen(n, m, c, blocks)
                for o in range(2):
                    weights[o].append(halves(received * last_scale[n, m, 2 * c + o]))
            for o in range(2):
                sums[o] = sums[o] + against(weights[o], n, m, o)
        for o in range(2):
            last_total[o] += sums[o]

    def emit():
        for o in range(2):
            signal = jnp.zeros((1, NBIN), jnp.float32)
            for q in range(8):
                if q % 4 < 3:
                    rows = [(16 * g + q, 16 * g + 8 + q) for g in range(4)]
                    source = total
                else:
                    rows = [(2 * g + q // 4, 8 + 2 * g + q // 4) for g in range(4)]
                    source = last_total
                whole = jnp.concatenate([source[o, h : h + 1, :] + source[o, l : l + 1, :] for h, l in rows], 1)
                offset = q % 4 + q // 4
                signal = signal + (pltpu.roll(whole, offset, 1) if offset else whole)
            signal_ref[o : o + 1, :] = signal

    total[...] = jnp.zeros_like(total)
    last_total[...] = jnp.zeros_like(last_total)
    for load in loads[:7]:
        load.wait()
    for t in range(CT):
        weight[0:NV, t * CZ : (t + 1) * CZ] = fw_ref[:, t, :]
    rows = jnp.concatenate([list_ref[...], count_ref[...], jnp.zeros((3, NR), jnp.int32)], 0).astype(jnp.float32)
    places = lax.broadcasted_iota(jnp.int32, (8, NR), 0) == lax.broadcasted_iota(jnp.int32, (8, NR), 1)
    list_out[...] = lax.dot_general(
        rows,
        places.astype(jnp.float32),
        (((0,), (0,)), ((), ())),
        precision=lax.Precision.HIGHEST,
        preferred_element_type=jnp.float32,
    )
    sample(0)
    pl.semaphore_wait(barrier, jnp.where(interface, NA - 1 + NB - 1 + NA, NA - 1 + NB - 1))
    send_edges(0)
    list_first()
    def between(k):
        if k == 0:
            for load in loads[7:]:
                load.wait()

        @pl.loop(2 * k, 2 * k + 2)
        def _(n):
            prepare(n)

        if k == 2:
            list_wait()
            widen()
        if k == 3:
            line_start(2)
            pair_start(1)
        down, up = theta_copies(k)
        down.wait_recv()
        up.wait_recv()

    for k in range(4):
        @pl.loop(0, CT)
        def _(step):
            if k == free:
                @pl.when(step == CT // 2)
                def _():
                    relay()

            @pl.when(step == CT - 2)
            def _():
                between(k)

            plane(k, lax.rem(step + 1, CT))

        land(k)
        correct(k)
        if k < 3:
            send_edges(k + 1)
        if k == 0:
            sample(1)
            ring_start(0)
            list_second()
        elif k == 1:
            sample(2)
            ring_start(1)
            line_start(0)
        elif k == 2:
            sample(3)
            ring_start(2)
            line_start(1)
            pair_start(0)

    for which in range(2):
        pair_copy(which).wait_recv()

    @pl.loop(0, NB)
    def _(n):
        @pl.when(n == NB // 2)
        def _():
            pair_start(2)

        bin_first(n)

    pair_copy(2).wait_recv()

    @pl.loop(0, NB)
    def _(n):
        bin_last(n)

    emit()
    for which in range(3):
        wait_rows(gathers[which].at[0, 0, pl.ds(0, NA // 2 - 1)], ring_send.at[which])
        wait_rows(gathers[which].at[pl.ds(0, NB - 1), 0], line_send.at[which])
        pair_copy(which).wait_send()
    for k in range(4):
        down, up = theta_copies(k)
        down.wait_send()
        up.wait_send()
        down, up = axial_copies(k)

        @pl.when(has_lo)
        def _():
            down.wait_send()

        @pl.when(has_hi)
        def _():
            up.wait_send()

        @pl.when(interface)
        def _():
            if k == free:
                wait_rows(row_out.at[k], row_send.at[k])
                wait_rows(row_sel.at[pl.ds(0, NA - 1)], sel_send.at[0])
            else:
                wait_rows(near[k].at[pl.ds(0, 56), pl.ds(0, NV), :], row_send.at[k])


def step_call(
    free, x, damping, jacobians, face_weight, phase_shift, lists, counts, bins, fractions, gains
):
    vmem = pl.BlockSpec(memory_space=pltpu.VMEM)
    hbm = pl.BlockSpec(memory_space=pltpu.HBM)
    state = pltpu.VMEM((NV, PAD, NR), jnp.float32)
    edge = pltpu.VMEM((4, NV, CT, NR), jnp.float32)
    row = pltpu.VMEM((NA, PIECE, NR), jnp.float32)
    dma = pltpu.SemaphoreType.DMA
    return pl.pallas_call(
        functools.partial(step_kernel, free),
        out_shape=(
            jax.ShapeDtypeStruct((NV, ROWS, NR), jnp.float32),
            jax.ShapeDtypeStruct((2, NBIN), jnp.float32),
        ),
        in_specs=[hbm] * 10,
        out_specs=(vmem,) * 2,
        scratch_shapes=[
            pltpu.VMEM((NB, NA, NR), jnp.float32),
            pltpu.VMEM((NB, 2, NA // 2, 8, NR), jnp.float32),
            pltpu.VMEM((NB, 2, NA // 2, 4, NR), jnp.float32),
            pltpu.VMEM((NB, 2, NA // 2, 4, NR), jnp.float32),
            pltpu.VMEM((NA, NB, PIECE, 128), jnp.int32),
            pltpu.VMEM((NA, NB, PIECE, 128), jnp.float32),
            pltpu.VMEM((NA, NB, PIECE, 128), jnp.float32),
            pltpu.VMEM((NB, NA, 2, 32, 512), jnp.bfloat16),
            pltpu.VMEM((NB, NA, PIECE, 8, 128), jnp.float32),
            pltpu.VMEM((NB, NA, PIECE, 8, 128), jnp.float32),
            pltpu.VMEM((NB, NA, 5 * 128), jnp.float32),
            pltpu.VMEM((2, 64, 32), jnp.float32),
            pltpu.VMEM((2, 16, 32), jnp.float32),
            pltpu.VMEM((ROWS, NR), jnp.float32),
            pltpu.SMEM((NV, 3, NV), jnp.float32),
            pltpu.VMEM((NV, CT, CZ), jnp.float32),
            pltpu.SMEM((4,), jnp.int32),
            pltpu.VMEM((4, NR), jnp.int32),
            pltpu.VMEM((1, NR), jnp.int32),
            pltpu.VMEM((8, ROWS), jnp.float32),
        ]
        + [state] * 4
        + [edge] * 4
        + [pltpu.VMEM((4, CT, PIECE, NR), jnp.float32), row, row, row]
        + [pltpu.VMEM((64, PIECE, NR), jnp.float32)] * 3
        + [pltpu.VMEM((CT * PIECE, NR), jnp.float32)]
        + [pltpu.VMEM((NA * NB, NR), jnp.float32)] * 2
        + [pltpu.VMEM((NB, NA, NR), jnp.float32)]
        + [pltpu.VMEM((rows, NR), jnp.float32) for rows in (8, 4, 4)]
        + [dma((10,)), dma((4, 2)), dma((4, 2)), dma((4, 2)), dma((4, 2))]
        + [dma((4,)), dma((4,)), dma((1,)), dma((1,))]
        + [dma((2,))] * 2
        + [dma((3,))] * 6,
        compiler_params=pltpu.CompilerParams(
            collective_id=free, has_side_effects=True, vmem_limit_bytes=44 << 20
        ),
        name="substeps%d" % free,
    )(x, damping, jacobians, face_weight, phase_shift, lists, counts, bins, fractions, gains)


def settle_kernel(state_ref, signal_ref, state_hbm, signal_hbm, sem):
    copies = [pltpu.make_async_copy(signal_ref, signal_hbm, sem.at[NV])]
    copies += [pltpu.make_async_copy(state_ref.at[v], state_hbm.at[v], sem.at[v]) for v in range(NV)]
    for copy in copies:
        copy.start()
    for copy in copies:
        copy.wait()


def settle(state, signal):
    vmem = pl.BlockSpec(memory_space=pltpu.VMEM)
    hbm = pl.BlockSpec(memory_space=pltpu.HBM)
    return pl.pallas_call(
        settle_kernel,
        out_shape=(
            jax.ShapeDtypeStruct((NV, ROWS, NR), jnp.float32),
            jax.ShapeDtypeStruct((2, NBIN), jnp.float32),
        ),
        in_specs=[vmem, vmem],
        out_specs=(hbm, hbm),
        scratch_shapes=[pltpu.SemaphoreType.DMA((NV + 1,))],
        compiler_params=pltpu.CompilerParams(vmem_limit_bytes=4 << 20),
        name="settle",
    )(state, signal)


def free_kernel(shift_hbm, out_ref, shift_ref, sem):
    copy = pltpu.make_async_copy(shift_hbm, shift_ref, sem.at[0])
    copy.start()
    copy.wait()
    flags = []
    for k in range(4):
        r = shift_ref[k]
        flags.append((r == 0, r == CT * NA - 1, jnp.logical_and(r >= 128, r < 144)))

    def settled(k):
        others = [flags[n] for n in range(4) if n != k]
        found = [others[0][f] | others[1][f] | others[2][f] for f in range(3)]
        return found[0] & found[1] & found[2]

    out_ref[0] = jnp.where(settled(0), 0, jnp.where(settled(1), 1, jnp.where(settled(2), 2, 3)))


def free_substep(phase_shift):
    return pl.pallas_call(
        free_kernel,
        out_shape=jax.ShapeDtypeStruct((1,), jnp.int32),
        in_specs=[pl.BlockSpec(memory_space=pltpu.HBM)],
        out_specs=pl.BlockSpec(memory_space=pltpu.SMEM),
        scratch_shapes=[pltpu.SMEM((4,), jnp.int32), pltpu.SemaphoreType.DMA((1,))],
        name="free_substep",
    )(phase_shift)[0]


def local(
    flow_state,
    damping,
    jacobians,
    face_weight,
    phase_shift,
    face_list,
    face_count,
    arrival_bin,
    arrival_fraction,
    arrival_gain,
):
    free = free_substep(phase_shift)
    new_state, signal = lax.switch(
        free,
        [functools.partial(step_call, k) for k in range(4)],
        flow_state.reshape(NV, ROWS, NR),
        damping.reshape(ROWS, NR),
        jnp.transpose(jacobians, (1, 0, 2)),
        face_weight,
        phase_shift,
        face_list[0].T,
        face_count,
        arrival_bin.reshape(NA, NB, PIECE, 128),
        arrival_fraction.reshape(NA, NB, PIECE, 128),
        arrival_gain.reshape(NA, NB, PIECE, 128),
    )
    new_state, signal = settle(new_state, signal)
    return new_state.reshape(NV, CT, CZ, NR), signal


def solution(mesh):
    return jax.shard_map(
        local,
        mesh=mesh,
        in_specs=(
            P(None, "sector", "axial", None),
            P("sector", "axial", None),
            P(),
            P(None, "sector", "axial"),
            P(),
            P(("sector", "axial"), None, None),
            P(("sector", "axial"), None),
            P(("sector", "axial"), None, None, None, None),
            P(("sector", "axial"), None, None, None, None),
            P(("sector", "axial"), None, None, None, None),
        ),
        out_specs=(P(None, "sector", "axial", None), P(("sector", "axial"), None)),
        check_vma=False,
    )
```
